128 devices in a mesh: span: 16 (over x, y), expert: 8 (over z, core).
Axes of the slice: x: 4, y: 4, z: 4, core: 2. Of those that a mesh axis runs over, the one named last changes fastest.
Arguments:
- residual_in: bfloat16 [16384, 6144], P(('span', 'expert')), may hold values from -6 to 6
- queries: bfloat16 [16384, 4096], P('span', 'expert'), may hold values from -6 to 6
- key_rows: bfloat16 [16384, 4096], P('span', 'expert'), may hold values from -6 to 6
- values: bfloat16 [16384, 4096], P('span', 'expert'), may hold values from -6 to 6
- log_keep: float32 [16384, 32], P('span', 'expert'), may hold values from -0.52 to 0, as said below
- prompt_start: int32 [16], P('span'), may hold values from 1 to 1024, as said below
- out_proj: bfloat16 [4096, 6144], P('expert', 'span'), may hold values from -0.09375 to 0.09375
- norm_gain: float32 [6144], replicated, may hold values from 0.1 to 1.9
- expert_ids: int32 [16384, 1], P(('span', 'expert')), may hold values from 0 to 15; in each aligned block of 128 rows (0 to 127, 128 to 255, ...) at most 10 rows name the same one
- w_gate: bfloat16 [16, 6144, 5120], P('span', None, 'expert'), may hold values from -0.078125 to 0.078125
- w_up: bfloat16 [16, 6144, 5120], P('span', None, 'expert'), may hold values from -0.078125 to 0.078125
Outputs:
- hidden_state: bfloat16 [16384, 6144], P(('span', 'expert'))
- expert_hidden: bfloat16 [16, 1280, 5120], P('span', None, 'expert')
The draws below stay inside these ranges and needn't reach their ends.
Inputs may be any that keep to these rules, and one draw needn't show every extreme that they name: `log_keep`: logarithm of a share of state kept, always below 0. `prompt_start`: position within its section of 1024 tokens at which a new prompt begins, 1024 where none does; exactly one section of the upper half of the 16 sections holds such a start. `expert_ids`: at most 10 of the 128 rows of one device name the same expert, and in every draw some device has exactly 10 rows naming one expert.
All inputs are finite; a program needn't handle non-finite values.
Results may differ from the reference program's by a relative error of at most 0.029.
Values may be sent and summed in bfloat16 or wider, within the bound.
No kernel may reach another device: no remote copies, remote signals or barrier semaphores. Data moves between devices by JAX's collectives and lax.ppermute only.
A program may use at most 192 MiB of HBM per device.

```python
import math
import jax
import jax.numpy as jnp
import numpy as np
from jax import lax

D = 6144
LOCAL_HEADS = 32
HEAD = 128
FF_WIN = 5120
BLK = 512
TOK = 128
TC = 1024
WINDOW_TOKENS = 16384
EXPERTS = 16
CAP = 10
ROWS = 1280
N_SPAN = 16
N_EXPERT = 8


def draw_log_keep(key, part):
    parallel_flows = jax.random.split(key, 7)
    slow_share = 0.5
    slow_heads = jax.random.uniform(parallel_flows[0], (LOCAL_HEADS,)) < slow_share
    fast_rate = jnp.exp(jax.random.uniform(parallel_flows[1], (LOCAL_HEADS,), minval=math.log(1.0 / 50.0), maxval=math.log(1.0 / 30.0)))
    slow_rate = jax.random.uniform(parallel_flows[2], (LOCAL_HEADS,), minval=0.1, maxval=0.4) / WINDOW_TOKENS
    head_rate = jnp.where(slow_heads, slow_rate, fast_rate)
    section_factor = jnp.exp(jax.random.uniform(parallel_flows[3], (WINDOW_TOKENS // TC, 1, LOCAL_HEADS), minval=-0.69, maxval=0.69))
    roughness = jax.random.uniform(parallel_flows[4], (WINDOW_TOKENS // TC, TC, LOCAL_HEADS), minval=0.5, maxval=1.5)
    logarithm_rows = -(head_rate * section_factor * roughness).reshape(WINDOW_TOKENS, LOCAL_HEADS)
    spike_places = jax.random.randint(parallel_flows[5], (2,), 0, WINDOW_TOKENS)
    spike_level = jnp.log(jax.random.uniform(parallel_flows[6], (2, LOCAL_HEADS), minval=0.6, maxval=0.8))
    token_places = jnp.arange(WINDOW_TOKENS)[:, None]
    logarithm_rows = jnp.where(token_places == spike_places[1], spike_level[1][None, :], logarithm_rows)
    logarithm_rows = jnp.where(token_places == spike_places[0], spike_level[0][None, :], logarithm_rows)
    return logarithm_rows.astype(jnp.float32)


def draw_prompt_start(key, part):
    parallel_flows = jax.random.split(key, 2)
    section_total = WINDOW_TOKENS // TC
    chosen_section = jax.random.randint(parallel_flows[0], (), section_total // 2, section_total)
    start_point = jax.random.randint(parallel_flows[1], (), 1, TC)
    return jnp.where(jnp.arange(section_total) == chosen_section, start_point, TC).astype(jnp.int32)


def levels(rng, shape, cuts, smallest, high):
    factor_of = 1.0
    for position, shards_of in cuts:
        draws = jax.random.uniform(jax.random.fold_in(jax.random.fold_in(rng, 6), position), (shards_of,), jnp.float32, smallest / len(cuts), high / len(cuts))
        factor_of = factor_of * jnp.repeat(jnp.exp(draws), shape[position] // shards_of).reshape((-1,) + (1,) * (len(shape) - 1 - position))
    return factor_of


def routed_block(rng, own, number, rows, amount, top, bound, skew):
    sequence = jax.random.permutation(rng, amount)
    crowded, common = portions_of(amount, rows * top, bound, skew, True), portions_of(amount, rows * top, bound, skew, False)
    places = jnp.arange(amount)

    def named(tallies, rotation):
        used = int((tallies > 0).sum())
        fixed = max(1, used // 4)
        passed = fixed + (places - fixed + rotation * (used - fixed)) % max(1, amount - fixed)
        return jnp.zeros((amount,), jnp.int32).at[sequence[jnp.where(places < fixed, places, passed)]].set(jnp.asarray(tallies, jnp.int32))

    tallies = jnp.where(number % 4 == 0, named(crowded, number // 4), named(common, number - number // 4 - 1))
    mixed = jax.random.permutation(jax.random.fold_in(own, 3), amount)
    source_of, receiver = mixed[0:amount // 2 * 2:2], mixed[1:amount // 2 * 2:2]
    slack = jnp.minimum(tallies[source_of] - 1, bound - tallies[receiver]) // 2
    slack = jnp.where((source_of == sequence[0]) | (receiver == sequence[0]) | (tallies[receiver] == 0), 0, jnp.maximum(slack, 0))
    passed = jax.random.randint(jax.random.fold_in(own, 4), (amount // 2,), 0, 1 << 20) % (slack + 1)
    tallies = tallies.at[source_of].add(-passed).at[receiver].add(passed)
    members = jnp.searchsorted(jnp.cumsum(tallies), jnp.arange(rows * top), side="right").astype(jnp.int32)
    grid = members.reshape(top, rows).T
    grid = grid[jax.random.permutation(jax.random.fold_in(own, 1), rows)]
    rotation = jax.random.randint(jax.random.fold_in(own, 2), (rows, 1), 0, top)
    return jnp.take_along_axis(grid, (jnp.arange(top)[None, :] + rotation) % top, axis=1)


def portions_of(number_of, total, limit, lean, full):
    weights = [(1 << 20) // math.isqrt(standing ** lean) + 1 for standing in range(1, number_of + 1)]
    largest = limit if full else min(limit, max(-(-total // number_of), total * weights[0] // sum(weights)))
    least = 1 if total - largest >= number_of - 1 else 0
    counts, surplus = [largest] + [least] * (number_of - 1), total - largest - least * (number_of - 1)
    while surplus > 0:
        movable = [i for i in range(1, number_of) if counts[i] < largest] or [i for i in range(1, number_of) if counts[i] < limit]
        mass, remaining = sum([weights[i] for i in movable]), surplus
        for i in movable:
            addition = min(limit - counts[i], max(1, remaining * weights[i] // mass), surplus)
            counts[i] = counts[i] + addition
            surplus = surplus - addition
    return np.array(counts)


def scatter_about(own_key, shape, deviation, limit, pieces=(), held_as=jnp.bfloat16):
    gain = levels(own_key, shape, pieces, -0.22, 0.18) if pieces else 1.0
    values = jax.random.normal(own_key, shape, jnp.float32) * deviation * gain
    return jnp.minimum(jnp.maximum(values, -limit), limit).astype(held_as)


def setup_inputs(seed: int = 0) -> dict:
    streams_of = jax.random.split(jax.random.key(seed), 12)
    residual_in = scatter_about(streams_of[0], (WINDOW_TOKENS, D), 1.0, 6.0, ((0, 128),))
    queries = scatter_about(streams_of[1], (WINDOW_TOKENS, LOCAL_HEADS * HEAD), 1.0, 6.0, ((0, 16), (1, 8)))
    key_rows = scatter_about(streams_of[2], (WINDOW_TOKENS, LOCAL_HEADS * HEAD), 1.0, 6.0, ((0, 16), (1, 8)))
    values = scatter_about(streams_of[3], (WINDOW_TOKENS, LOCAL_HEADS * HEAD), 1.0, 6.0, ((0, 16), (1, 8)))
    log_keep = draw_log_keep(jax.random.fold_in(streams_of[11], 71), 0)
    prompt_start = draw_prompt_start(jax.random.fold_in(streams_of[11], 71), 0)
    out_proj = scatter_about(streams_of[6], (LOCAL_HEADS * HEAD, D), (LOCAL_HEADS * HEAD) ** -0.5, 0.09375, ((0, 8), (1, 16)))
    norm_gain = jnp.clip(1.0 + 0.18 * jax.random.normal(streams_of[7], (D,), jnp.float32), 0.1, 1.9)
    expert_ids_keys = jax.random.split(jax.random.fold_in(streams_of[8], 1), WINDOW_TOKENS // TOK)
    expert_ids_turns = jax.random.permutation(jax.random.fold_in(streams_of[8], 3), WINDOW_TOKENS // TOK)
    expert_ids = jax.vmap(lambda own, number: routed_block(jax.random.fold_in(streams_of[8], 2), own, number, TOK, EXPERTS, 1, CAP, 2))(expert_ids_keys, expert_ids_turns).reshape((WINDOW_TOKENS, 1))
    w_gate = scatter_about(streams_of[9], (EXPERTS, D, FF_WIN), D ** -0.5, 0.078125, ((0, 16), (2, 8)))
    w_up = scatter_about(streams_of[10], (EXPERTS, D, FF_WIN), D ** -0.5, 0.078125, ((0, 16), (2, 8)))
    return {"residual_in": residual_in, "queries": queries, "key_rows": key_rows, "values": values, "log_keep": log_keep, "prompt_start": prompt_start, "out_proj": out_proj, "norm_gain": norm_gain, "expert_ids": expert_ids, "w_gate": w_gate, "w_up": w_up}


EPSILON = 1e-05
HIGHEST = lax.Precision.HIGHEST

def block_pass(carried, block_in):
    queries, key_rows, values, log_keep, doc_count, base_count = block_in
    cumulative = jnp.cumsum(log_keep, axis=0)
    cum_heads = cumulative.T
    token_places = jnp.arange(log_keep.shape[0])
    allowed = (token_places[:, None] >= token_places[None, :]) & (doc_count[:, None] == doc_count[None, :])
    allowed = allowed[None, :, :]
    spread = cum_heads[:, :, None] - cum_heads[:, None, :]
    decay_factor = jnp.where(allowed, jnp.exp(jnp.where(allowed, spread, 0.0)), 0.0)
    query_f = queries.astype(jnp.float32)
    key_f = key_rows.astype(jnp.float32)
    value_f = values.astype(jnp.float32)
    scores = jnp.einsum('thd,shd->hts', query_f, key_f)
    weights = (scores * decay_factor).astype(jnp.bfloat16)
    intra_part = jnp.einsum('hts,she->the', weights.astype(jnp.float32), value_f)
    opened = jnp.where((doc_count == base_count)[:, None], jnp.exp(cumulative), 0.0)
    incoming = jnp.einsum('thd,hde->the', query_f, carried, precision=HIGHEST) * opened[:, :, None]
    last_count = doc_count[-1]
    tail_weight = jnp.where((doc_count == last_count)[:, None], jnp.exp(cumulative[-1][None, :] - cumulative), 0.0)
    through = jnp.where(last_count == base_count, jnp.exp(cumulative[-1]), 0.0)
    added_state = jnp.einsum('shd,she->hde', key_f * tail_weight[:, :, None], value_f, precision=HIGHEST)
    return (carried * through[:, None, None] + added_state, intra_part + incoming)

def reference(residual_in, queries, key_rows, values, log_keep, prompt_start, out_proj, norm_gain, expert_ids, w_gate, w_up):
    token_places = jnp.arange(WINDOW_TOKENS).astype(jnp.int32)
    section_ids = jnp.arange(N_SPAN).astype(jnp.int32)
    has_start = prompt_start < TC
    starts = section_ids * TC + prompt_start
    doc_count = lax.optimization_barrier(jnp.sum(((token_places[:, None] >= starts[None, :]) & has_start[None, :]).astype(jnp.int32), axis=1))
    block_total = WINDOW_TOKENS // BLK
    base_count = jnp.concatenate([jnp.zeros((1,), jnp.int32), doc_count[BLK - 1::BLK][:-1].astype(jnp.int32)])
    query_blocks = queries.reshape(block_total, BLK, LOCAL_HEADS, HEAD)
    key_blocks = key_rows.reshape(block_total, BLK, LOCAL_HEADS, HEAD)
    value_blocks = values.reshape(block_total, BLK, LOCAL_HEADS, HEAD)
    keep_blocks = log_keep.reshape(block_total, BLK, LOCAL_HEADS)
    count_blocks = doc_count.reshape(block_total, BLK)
    start_state = jnp.zeros((LOCAL_HEADS, HEAD, HEAD), jnp.float32)
    final_state, outputs = lax.scan(block_pass, start_state, (query_blocks, key_blocks, value_blocks, keep_blocks, count_blocks, base_count))
    attn_heads = outputs.reshape(WINDOW_TOKENS, LOCAL_HEADS, HEAD)
    normed = attn_heads * lax.rsqrt(lax.optimization_barrier(jnp.mean(attn_heads * attn_heads, axis=2, keepdims=True)) + EPSILON)
    normed = normed.astype(jnp.bfloat16).reshape(WINDOW_TOKENS, LOCAL_HEADS * HEAD)
    group_width = LOCAL_HEADS * HEAD // N_EXPERT
    attn_sum = jnp.zeros((WINDOW_TOKENS, D), jnp.float32)
    for group_index in range(N_EXPERT):
        lower_edge = group_index * group_width
        upper_edge = lower_edge + group_width
        partial_value = jnp.dot(normed[:, lower_edge:upper_edge], out_proj[lower_edge:upper_edge], preferred_element_type=jnp.float32)
        rounded = lax.optimization_barrier(partial_value.astype(jnp.bfloat16))
        attn_sum = attn_sum + rounded.astype(jnp.float32)
    mixed = residual_in.astype(jnp.float32) + attn_sum
    hidden_state = mixed.astype(jnp.bfloat16)
    moe_in = (mixed * lax.rsqrt(lax.optimization_barrier(jnp.mean(mixed * mixed, axis=1, keepdims=True)) + EPSILON) * norm_gain).astype(jnp.bfloat16)
    chosen = expert_ids[:, 0]
    onehot = (chosen[:, None] == jnp.arange(EXPERTS)[None, :]).astype(jnp.int32).reshape(WINDOW_TOKENS // TOK, TOK, EXPERTS)
    earlier_count = jnp.cumsum(onehot, axis=1) - onehot
    slot_index = lax.optimization_barrier(jnp.sum(earlier_count * onehot, axis=2)).reshape(WINDOW_TOKENS).astype(jnp.int32)
    source_block = token_places // TOK
    row_index = (source_block % N_EXPERT * (N_SPAN * CAP) + source_block // N_EXPERT * CAP + slot_index).astype(jnp.int32)

    def one_expert(operands):
        expert_index, gate_w, up_w = operands
        target = jnp.where(chosen == expert_index, row_index, ROWS).astype(jnp.int32)
        buffer_rows = jnp.zeros((ROWS, D), jnp.bfloat16).at[target].set(moe_in, mode='drop')
        gate_part = jnp.dot(buffer_rows, gate_w, preferred_element_type=jnp.float32)
        up_part = jnp.dot(buffer_rows, up_w, preferred_element_type=jnp.float32)
        return (jax.nn.silu(gate_part) * up_part).astype(jnp.bfloat16)
    expert_hidden = lax.map(one_expert, (jnp.arange(EXPERTS).astype(jnp.int32), w_gate, w_up))
    return (hidden_state, expert_hidden)
```

```python
import functools

import jax
import jax.numpy as jnp
from jax import lax
from jax.experimental import pallas as pl
from jax.experimental.pallas import tpu as pltpu
from jax.sharding import PartitionSpec as P

BLK = 512
EPSILON = 1e-05
HIGHEST = lax.Precision.HIGHEST
F32 = jnp.float32
BF16 = jnp.bfloat16
VMEM_LIMIT = 56 * 1024 * 1024
HEADS = 4
HD = 128
GRID_SIDE = 4


def whole(shape):
    return pl.BlockSpec(shape, lambda *_: (0,) * len(shape))


def smem():
    return pl.BlockSpec(memory_space=pltpu.SMEM)


def split_dot(a_f32, b_bf16):
    high = a_f32.astype(BF16)
    low = (a_f32 - high.astype(F32)).astype(BF16)
    return jnp.dot(high, b_bf16, preferred_element_type=F32) + jnp.dot(
        low, b_bf16, preferred_element_type=F32
    )


def state_kernel(start_ref, k_ref, v_ref, keep_ref, pay_ref, first_ref, thr_ref, cum_ref):
    start = start_ref[0]
    blocks = k_ref.shape[0] // BLK
    row = lax.broadcasted_iota(jnp.int32, (BLK, BLK), 0)
    col = lax.broadcasted_iota(jnp.int32, (BLK, BLK), 1)
    lower = (row >= col).astype(F32)
    place = lax.broadcasted_iota(jnp.int32, (BLK, HD), 0)
    through, tails = [], []
    for b in range(blocks):
        own = pl.ds(b * BLK, BLK)
        cum = jnp.dot(lower, keep_ref[own, :], precision=HIGHEST, preferred_element_type=F32)
        cum_ref[own, :] = cum
        end = cum[BLK - 1 :, :]
        here = start - b * BLK
        same = (place >= here) == (here <= BLK - 1)
        tails.append(jnp.where(same, jnp.exp(end - cum), 0.0))
        resets = (here >= 0) & (here < BLK)
        through.append(jnp.where(resets, 0.0, jnp.exp(end)))
    pay_ref[HEADS * HD :, :] = jnp.zeros_like(pay_ref[HEADS * HD :, :])
    thr_ref[...] = jnp.zeros_like(thr_ref)
    highs, lows = [], []
    for h in range(HEADS):
        lanes = slice(h * HD, (h + 1) * HD)
        state = None
        passed = jnp.ones((1, HD), F32)
        for b in range(blocks):
            own = pl.ds(b * BLK, BLK)
            key = k_ref[own, lanes].astype(F32) * tails[b][:, h : h + 1]
            added = split_dot(key.T, v_ref[own, lanes])
            thr = jnp.broadcast_to(through[b][:, h : h + 1], (1, HD))
            passed = passed * thr
            if b == 0:
                first_ref[lanes, :] = added
                thr_ref[h : h + 1, :] = thr
                state = added
            else:
                state = state * thr + added
        pay_ref[lanes, :] = state.astype(BF16)
        high = passed.astype(BF16)
        highs.append(high.astype(F32))
        lows.append(passed - high.astype(F32))
    none = jnp.zeros((8 - HEADS, HD), F32)
    pay_ref[HEADS * HD :, :] = jnp.concatenate(
        highs + [none] + lows + [none], axis=0
    ).astype(BF16)


def local_state(start, key_rows, values, keep_pad):
    tokens, width = key_rows.shape
    return pl.pallas_call(
        state_kernel,
        grid=(1,),
        in_specs=[smem(), whole((tokens, width)), whole((tokens, width)), whole((tokens, HD))],
        out_specs=[
            whole((width + 16, HD)),
            whole((width, HD)),
            whole((8, HD)),
            whole((tokens, HD)),
        ],
        out_shape=[
            jax.ShapeDtypeStruct((width + 16, HD), BF16),
            jax.ShapeDtypeStruct((width, HD), F32),
            jax.ShapeDtypeStruct((8, HD), F32),
            jax.ShapeDtypeStruct((tokens, HD), F32),
        ],
        compiler_params=pltpu.CompilerParams(vmem_limit_bytes=VMEM_LIMIT),
        cost_estimate=pl.CostEstimate(
            flops=2 * 10**9, bytes_accessed=4 * 10**6, transcendentals=10**5
        ),
        name="local_state",
    )(start, key_rows, values, keep_pad)


def intra_kernel(start_ref, q_ref, k_ref, v_ref, cum_ref, keep_t_ref, out_ref):
    start = start_ref[0]
    blocks = q_ref.shape[0] // BLK
    row = lax.broadcasted_iota(jnp.int32, (BLK, BLK), 0)
    col = lax.broadcasted_iota(jnp.int32, (BLK, BLK), 1)
    upper = (row <= col).astype(F32)
    part = BLK // 2
    for b in range(blocks):
        cum_t = jnp.dot(
            keep_t_ref[:, b * BLK : (b + 1) * BLK],
            upper,
            precision=HIGHEST,
            preferred_element_type=F32,
        )
        here = start - b * BLK
        for r in range(2):
            lo, n = r * part, (r + 1) * part
            t = lax.broadcasted_iota(jnp.int32, (part, n), 0) + lo
            s = lax.broadcasted_iota(jnp.int32, (part, n), 1)
            allowed = (t >= s) & ((s >= here) | (t < here))
            rows = pl.ds(b * BLK + lo, part)
            for h in range(HEADS):
                lanes = slice(h * HD, (h + 1) * HD)
                scores = lax.dot_general(
                    q_ref[rows, lanes],
                    k_ref[b * BLK : b * BLK + n, lanes],
                    (((1,), (1,)), ((), ())),
                    preferred_element_type=F32,
                )
                spread = cum_ref[rows, h : h + 1] - cum_t[h : h + 1, :n]
                decay = jnp.where(allowed, jnp.exp(jnp.where(allowed, spread, 0.0)), 0.0)
                weights = (scores * decay).astype(BF16)
                out_ref[rows, lanes] = jnp.dot(
                    weights, v_ref[b * BLK : b * BLK + n, lanes], preferred_element_type=F32
                )


def intra_part(start, queries, key_rows, values, cum, keep_t):
    tokens, width = queries.shape
    return pl.pallas_call(
        intra_kernel,
        grid=(1,),
        in_specs=[
            smem(),
            whole((tokens, width)),
            whole((tokens, width)),
            whole((tokens, width)),
            whole((tokens, HD)),
            whole((8, tokens)),
        ],
        out_specs=whole((tokens, width)),
        out_shape=jax.ShapeDtypeStruct((tokens, width), F32),
        compiler_params=pltpu.CompilerParams(vmem_limit_bytes=VMEM_LIMIT),
        cost_estimate=pl.CostEstimate(
            flops=8 * 10**9, bytes_accessed=6 * 10**6, transcendentals=2 * 10**6
        ),
        name="intra_part",
    )(start, queries, key_rows, values, cum, keep_t)


def passes_of(pay, h):
    base = HEADS * HD
    high = pay[base + h : base + h + 1, :].astype(F32)
    low = pay[base + 8 + h : base + 9 + h, :].astype(F32)
    return high + low


def row_kernel(place_ref, p0, p1, p2, p3, pay_ref, prefix_ref, through_ref):
    own = place_ref[0]
    parts = [p[...] for p in (p0, p1, p2, p3)]
    places = [lax.rem(own - d + GRID_SIDE, GRID_SIDE) for d in range(GRID_SIDE)]
    one = jnp.ones((1, HD), F32)
    through_ref[...] = jnp.zeros_like(through_ref)
    highs, lows = [], []
    for h in range(HEADS):
        lanes = slice(h * HD, (h + 1) * HD)
        thr = [passes_of(p, h) for p in parts]
        total = jnp.zeros((HD, HD), F32)
        prefix = jnp.zeros((HD, HD), F32)
        passed, before = one, one
        for d in range(GRID_SIDE):
            after, between = one, one
            for e in range(GRID_SIDE):
                if e == d:
                    continue
                later = places[e] > places[d]
                after = after * jnp.where(later, thr[e], one)
                between = between * jnp.where(later & (places[e] < own), thr[e], one)
            state = parts[d][lanes, :].astype(F32)
            total = total + state * after
            prefix = prefix + state * jnp.where(places[d] < own, between, 0.0 * one)
            passed = passed * thr[d]
            before = before * jnp.where(places[d] < own, thr[d], one)
        pay_ref[lanes, :] = total.astype(BF16)
        prefix_ref[lanes, :] = prefix
        through_ref[h : h + 1, :] = before
        high = passed.astype(BF16)
        highs.append(high.astype(F32))
        lows.append(passed - high.astype(F32))
    none = jnp.zeros((8 - HEADS, HD), F32)
    pay_ref[HEADS * HD :, :] = jnp.concatenate(
        highs + [none] + lows + [none], axis=0
    ).astype(BF16)


def row_states(place, parts):
    shape = parts[0].shape
    width = HEADS * HD
    return pl.pallas_call(
        row_kernel,
        grid=(1,),
        in_specs=[smem()] + [whole(shape)] * 4,
        out_specs=[whole(shape), whole((width, HD)), whole((8, HD))],
        out_shape=[
            jax.ShapeDtypeStruct(shape, BF16),
            jax.ShapeDtypeStruct((width, HD), F32),
            jax.ShapeDtypeStruct((8, HD), F32),
        ],
        cost_estimate=pl.CostEstimate(
            flops=10**6, bytes_accessed=10**6, transcendentals=0
        ),
        name="row_states",
    )(place, *parts)


def finish_kernel(
    start_ref, q_ref, intra_ref, cum_ref, e1, e2, e3, prefix_ref, before_ref, first_ref, thr_ref, out_ref
):
    start = start_ref[0]
    blocks = q_ref.shape[0] // BLK
    rows1, rows2, rows3 = e1[...], e2[...], e3[...]
    place = lax.broadcasted_iota(jnp.int32, (BLK, HD), 0)
    factors = []
    for b in range(blocks):
        here = start - b * BLK
        opened = (place < here) | (here < 0)
        factors.append(jnp.where(opened, jnp.exp(cum_ref[pl.ds(b * BLK, BLK), :]), 0.0))
    for h in range(HEADS):
        lanes = slice(h * HD, (h + 1) * HD)
        far = rows2[lanes, :].astype(F32) + passes_of(rows2, h) * rows3[lanes, :].astype(F32)
        earlier = rows1[lanes, :].astype(F32) + passes_of(rows1, h) * far
        state = prefix_ref[lanes, :] + before_ref[h : h + 1, :] * earlier
        for b in range(blocks):
            own = pl.ds(b * BLK, BLK)
            if b > 0:
                state = state * thr_ref[h : h + 1, :] + first_ref[lanes, :]
            high = state.astype(BF16)
            low = (state - high.astype(F32)).astype(BF16)
            q = q_ref[own, lanes]
            carried = jnp.dot(q, high, preferred_element_type=F32) + jnp.dot(
                q, low, preferred_element_type=F32
            )
            heads = intra_ref[own, lanes] + carried * factors[b][:, h : h + 1]
            mean = jnp.mean(heads * heads, axis=1, keepdims=True)
            out_ref[own, lanes] = (heads * lax.rsqrt(mean + EPSILON)).astype(BF16)


def finish(start, queries, intra, cum, rows, prefix, before, first, thr):
    tokens, width = queries.shape
    pay = rows[0].shape
    return pl.pallas_call(
        finish_kernel,
        grid=(1,),
        in_specs=[
            smem(),
            whole((tokens, width)),
            whole((tokens, width)),
            whole((tokens, HD)),
            whole(pay),
            whole(pay),
            whole(pay),
            whole((width, HD)),
            whole((8, HD)),
            whole((width, HD)),
            whole((8, HD)),
        ],
        out_specs=whole((tokens, width)),
        out_shape=jax.ShapeDtypeStruct((tokens, width), BF16),
        compiler_params=pltpu.CompilerParams(vmem_limit_bytes=VMEM_LIMIT),
        cost_estimate=pl.CostEstimate(
            flops=10**9, bytes_accessed=5 * 10**6, transcendentals=10**6
        ),
        name="finish",
    )(start, queries, intra, cum, *rows, prefix, before, first, thr)


def proj_kernel(count, src_ref, *refs):
    xs = refs[:count]
    w_ref, res_ref, gain_ref, h_ref, x_ref = refs[count:]
    tile = 256

    def rows_of(step, _):
        own = pl.ds(pl.multiple_of(step * tile, tile), tile)
        total = jnp.zeros((tile, w_ref.shape[1]), F32)
        for c in range(count):
            depth = xs[c].shape[1]
            at = pl.ds(pl.multiple_of(src_ref[c] * depth, depth), depth)
            total = total + jnp.dot(
                xs[c][own, :], w_ref[at, :], preferred_element_type=F32
            )
        mixed = res_ref[own, :].astype(F32) + total
        h_ref[own, :] = mixed.astype(BF16)
        x_ref[own, :] = (mixed * gain_ref[...]).astype(BF16)
        return 0

    lax.fori_loop(0, res_ref.shape[0] // tile, rows_of, 0)


def project(src, xs, weights, res, gain):
    tokens = res.shape[0]
    columns = weights.shape[1]
    part = 256
    block = lambda rows: pl.BlockSpec((rows, part), lambda n, s: (0, n))
    return pl.pallas_call(
        functools.partial(proj_kernel, len(xs)),
        grid_spec=pltpu.PrefetchScalarGridSpec(
            num_scalar_prefetch=1,
            grid=(columns // part,),
            in_specs=[whole(x.shape) for x in xs]
            + [block(weights.shape[0]), block(tokens), block(1)],
            out_specs=[block(tokens), block(tokens)],
        ),
        out_shape=[jax.ShapeDtypeStruct((tokens, columns), BF16)] * 2,
        compiler_params=pltpu.CompilerParams(vmem_limit_bytes=VMEM_LIMIT),
        cost_estimate=pl.CostEstimate(
            flops=2 * tokens * columns * weights.shape[0],
            bytes_accessed=20 * 10**6,
            transcendentals=0,
        ),
        name="project",
    )(src, *xs, weights, res, gain)


def expert_kernel(count, begins, ends, src_ref, *refs):
    xs = refs[:count]
    gates = refs[count : 2 * count]
    ups = refs[2 * count : 3 * count]
    inverses = refs[3 * count : 4 * count]
    rest = refs[4 * count :]
    rows = xs[0].shape[0]
    if begins:
        gate = jnp.zeros((rows, gates[0].shape[1]), F32)
        up = jnp.zeros_like(gate)
        squares = jnp.zeros((rows, HD), F32)
    else:
        gate, up, squares = (r[...] for r in rest[:3])
        rest = rest[3:]
    for c in range(count):
        x = xs[c][...]
        gate = gate + jnp.dot(x, gates[c][...], preferred_element_type=F32)
        up = up + jnp.dot(x, ups[c][...], preferred_element_type=F32)
        plain = x.astype(F32) * inverses[c][...]
        plain = plain * plain
        for lane in range(plain.shape[1] // HD):
            squares = squares + plain[:, lane * HD : (lane + 1) * HD]
    if ends:
        mean = jnp.sum(squares, axis=1, keepdims=True) / ends
        scale = lax.rsqrt(mean + EPSILON)
        gate, up = gate * scale, up * scale
        rest[0][...] = (gate / (1.0 + jnp.exp(-gate)) * up).astype(BF16)
    else:
        rest[0][...] = gate
        rest[1][...] = up
        rest[2][...] = squares


def expert_part(src, xs, gate_w, up_w, inverse, carried, ends=0):
    tokens = xs[0].shape[0]
    hidden = gate_w.shape[1]
    tile = 320
    rows = lambda columns: pl.BlockSpec((tile, columns), lambda n, s: (n, 0))
    w_specs, i_specs = [], []
    for c, x in enumerate(xs):
        depth = x.shape[1]
        w_specs.append(pl.BlockSpec((depth, hidden), lambda n, s, c=c: (s[c], 0)))
        i_specs.append(pl.BlockSpec((1, depth), lambda n, s, c=c: (0, s[c])))
    kept = [rows(hidden), rows(hidden), rows(HD)]
    if ends:
        out_specs = rows(hidden)
        out_shape = jax.ShapeDtypeStruct((tokens, hidden), BF16)
    else:
        out_specs = kept
        out_shape = [
            jax.ShapeDtypeStruct((tokens, hidden), F32),
            jax.ShapeDtypeStruct((tokens, hidden), F32),
            jax.ShapeDtypeStruct((tokens, HD), F32),
        ]
    count = len(xs)
    return pl.pallas_call(
        functools.partial(expert_kernel, count, carried is None, ends),
        grid_spec=pltpu.PrefetchScalarGridSpec(
            num_scalar_prefetch=1,
            grid=(tokens // tile,),
            in_specs=[rows(x.shape[1]) for x in xs]
            + w_specs
            + w_specs
            + i_specs
            + ([] if carried is None else kept),
            out_specs=out_specs,
        ),
        out_shape=out_shape,
        compiler_params=pltpu.CompilerParams(vmem_limit_bytes=VMEM_LIMIT),
        cost_estimate=pl.CostEstimate(
            flops=4 * tokens * hidden * sum(x.shape[1] for x in xs),
            bytes_accessed=22 * 10**6,
            transcendentals=0,
        ),
        name="expert_part",
    )(
        src,
        *xs,
        *([gate_w] * count),
        *([up_w] * count),
        *([inverse] * count),
        *(() if carried is None else carried),
    )


def moved(block, axis, place_to):
    count = lax.axis_size(axis)
    return lax.ppermute(block, axis, [(i, place_to(i)) for i in range(count)])


def along(block, steps, cross=0):
    count = lax.axis_size("expert")
    return moved(block, "expert", lambda j: ((j // 2 + steps) * 2 + (j % 2 ^ cross)) % count)


def gathered(block, me):
    count = lax.axis_size("expert")
    other = me + 1 - 2 * lax.rem(me, 2)
    half = block.shape[1] // 2
    below, above = along(block, 1), along(block, -1)
    own_other = along(block, 0, 1)
    opp_a, opp_b = along(below[:, :half], 1), along(above[:, half:], -1)
    below_other, above_other = along(below, 0, 1), along(above, 0, 1)
    opp_a_other, opp_b_other = along(opp_a, 0, 1), along(opp_b, 0, 1)
    at = lambda j, d: lax.rem(j + d + count, count)
    first = [(block, me), (own_other, other)]
    second = [(below, at(me, -2)), (above, at(me, 2))]
    third = [(below_other, at(other, -2)), (above_other, at(other, 2))]
    opp, opp_other = at(me, 4), at(other, 4)
    fourth = [
        (opp_a, 2 * opp),
        (opp_b, 2 * opp + 1),
        (opp_a_other, 2 * opp_other),
        (opp_b_other, 2 * opp_other + 1),
    ]
    return first, second, third, fourth


def unzip(pairs):
    return [x for x, _ in pairs], jnp.stack([s for _, s in pairs]).astype(jnp.int32)


def on_device(
    residual_in,
    queries,
    key_rows,
    values,
    log_keep,
    prompt_start,
    out_proj,
    norm_gain,
    expert_ids,
    w_gate,
    w_up,
):
    tok_rows, model_width = residual_in.shape
    section_len = queries.shape[0]
    span_count = lax.axis_size("span")
    slice_count = lax.axis_size("expert")
    capacity = max(2, tok_rows * 5 // (4 * span_count))
    my_span = lax.axis_index("span")
    my_slice = lax.axis_index("expert")
    columns = model_width // slice_count

    half_rows = out_proj.shape[0] // 2
    parity = lax.rem(my_span, 2)
    send_a = lax.dynamic_slice_in_dim(out_proj, parity * half_rows, half_rows, 0)
    send_b = lax.dynamic_slice_in_dim(out_proj, (1 - parity) * half_rows, half_rows, 0)

    def route(flip):
        pairs = []
        for i in range(span_count):
            for j in range(slice_count):
                half = (i % 2) ^ flip
                pairs.append((i * slice_count + j, (2 * j + half) * slice_count + i // 2))
        return pairs

    got_a = lax.ppermute(send_a, ("span", "expert"), route(0))
    got_b = lax.ppermute(send_b, ("span", "expert"), route(1))
    piece = jnp.where(
        parity == 0,
        jnp.concatenate([got_a, got_b], axis=1),
        jnp.concatenate([got_b, got_a], axis=1),
    )
    proj_w = lax.all_gather(piece, "span", axis=0, tiled=True)

    keep_pad = jnp.pad(log_keep, ((0, 0), (0, HD - log_keep.shape[1])))
    keep_t = jnp.pad(log_keep.T, ((0, 8 - log_keep.shape[1]), (0, 0)))
    pay, first, thr, cum = local_state(prompt_start, key_rows, values, keep_pad)
    side = GRID_SIDE
    in_row = [
        moved(pay, "span", lambda i, d=d: i // side * side + (i + d) % side)
        for d in range(1, side)
    ]
    intra = intra_part(prompt_start, queries, key_rows, values, cum, keep_t)
    place = lax.rem(my_span, side)[None].astype(jnp.int32)
    row_pay, prefix, before = row_states(place, [pay] + in_row)
    rows = [
        lax.ppermute(
            row_pay,
            "span",
            [(i, i + d * side) for i in range(span_count) if i + d * side < span_count],
        )
        for d in range(1, side)
    ]
    normed = finish(prompt_start, queries, intra, cum, rows, prefix, before, first, thr)

    res = lax.all_to_all(residual_in, "expert", split_axis=1, concat_axis=0, tiled=True)
    ids = jnp.broadcast_to(expert_ids[:, 0][None, :], (slice_count, tok_rows))
    ids = lax.all_to_all(ids, "expert", split_axis=0, concat_axis=0, tiled=True)
    onehot = (ids[:, :, None] == jnp.arange(span_count)[None, None, :]).astype(BF16)
    earlier = jnp.tril(jnp.ones((tok_rows, tok_rows), BF16), -1)
    earlier_count = jnp.einsum("ts,bse->bte", earlier, onehot, preferred_element_type=F32)
    slot = jnp.sum(earlier_count * onehot.astype(F32), axis=2).astype(jnp.int32)
    block_of = jnp.arange(slice_count)[:, None]
    target = ((ids * slice_count + block_of) * capacity + slot).reshape(-1)
    slots = span_count * slice_count * capacity
    placing = (jnp.arange(slots)[:, None] == target[None, :]).astype(BF16)

    chunks = sum((list(g) for g in gathered(normed, my_slice)), [])
    xs, src = unzip(chunks)
    gain_cols = lax.dynamic_slice_in_dim(norm_gain, my_slice * columns, columns)[None, :]
    hidden_cols, rows_in = project(src, xs, proj_w, res, gain_cols)
    hidden_state = lax.all_to_all(
        hidden_cols, "expert", split_axis=0, concat_axis=1, tiled=True
    )

    packed = jnp.dot(placing, rows_in, preferred_element_type=F32).astype(BF16)
    packed = packed.reshape(span_count, slice_count * capacity, columns)
    arrived = lax.all_to_all(packed, "span", split_axis=0, concat_axis=0, tiled=True)
    arrived = arrived.reshape(slots, columns)
    inverse = (1.0 / norm_gain)[None, :]
    gate_w, up_w = w_gate[0], w_up[0]
    carried = None
    groups = gathered(arrived, my_slice)
    for number, group in enumerate(groups):
        xs, src = unzip(group)
        ends = model_width if number == len(groups) - 1 else 0
        carried = expert_part(src, xs, gate_w, up_w, inverse, carried, ends)
    r = jnp.arange(slots)
    block, rest = r // (span_count * capacity), r % (span_count * capacity)
    wanted = (rest // capacity * slice_count + block) * capacity + rest % capacity
    turning = (wanted[:, None] == r[None, :]).astype(BF16)
    hidden_rows = jnp.dot(turning, carried, preferred_element_type=F32).astype(BF16)
    return (hidden_state, hidden_rows[None])


def solution(mesh):
    placed = (
        P(("span", "expert"), None),
        P("span", "expert"),
        P("span", "expert"),
        P("span", "expert"),
        P("span", "expert"),
        P("span"),
        P("expert", "span"),
        P(),
        P(("span", "expert"), None),
        P("span", None, "expert"),
        P("span", None, "expert"),
    )
    return jax.shard_map(
        on_device,
        mesh=mesh,
        in_specs=placed,
        out_specs=(P(("span", "expert"), None), P("span", None, "expert")),
        check_vma=False,
    )
```

```python
import functools

import jax
import jax.numpy as jnp
from jax import lax
from jax.experimental import pallas as pl
from jax.experimental.pallas import tpu as pltpu
from jax.sharding import PartitionSpec as P

BLK = 512
EPSILON = 1e-05
HIGHEST = lax.Precision.HIGHEST
F32 = jnp.float32
BF16 = jnp.bfloat16
VMEM_LIMIT = 56 * 1024 * 1024
HEADS = 4
HD = 128
GRID_SIDE = 4


def whole(shape):
    return pl.BlockSpec(shape, lambda *_: (0,) * len(shape))


def smem():
    return pl.BlockSpec(memory_space=pltpu.SMEM)


def split_dot(a_f32, b_bf16):
    high = a_f32.astype(BF16)
    low = (a_f32 - high.astype(F32)).astype(BF16)
    return jnp.dot(high, b_bf16, preferred_element_type=F32) + jnp.dot(
        low, b_bf16, preferred_element_type=F32
    )


def state_kernel(start_ref, k_ref, v_ref, keep_ref, pay_ref, first_ref, thr_ref, cum_ref):
    start = start_ref[0]
    blocks = k_ref.shape[0] // BLK
    row = lax.broadcasted_iota(jnp.int32, (BLK, BLK), 0)
    col = lax.broadcasted_iota(jnp.int32, (BLK, BLK), 1)
    lower = (row >= col).astype(F32)
    place = lax.broadcasted_iota(jnp.int32, (BLK, HD), 0)
    through, tails = [], []
    for b in range(blocks):
        own = pl.ds(b * BLK, BLK)
        cum = jnp.dot(lower, keep_ref[own, :], precision=HIGHEST, preferred_element_type=F32)
        cum_ref[own, :] = cum
        end = cum[BLK - 1 :, :]
        here = start - b * BLK
        same = (place >= here) == (here <= BLK - 1)
        tails.append(jnp.where(same, jnp.exp(end - cum), 0.0))
        resets = (here >= 0) & (here < BLK)
        through.append(jnp.where(resets, 0.0, jnp.exp(end)))
    pay_ref[HEADS * HD :, :] = jnp.zeros_like(pay_ref[HEADS * HD :, :])
    thr_ref[...] = jnp.zeros_like(thr_ref)
    highs, lows = [], []
    for h in range(HEADS):
        lanes = slice(h * HD, (h + 1) * HD)
        state = None
        passed = jnp.ones((1, HD), F32)
        for b in range(blocks):
            own = pl.ds(b * BLK, BLK)
            key = k_ref[own, lanes].astype(F32) * tails[b][:, h : h + 1]
            added = split_dot(key.T, v_ref[own, lanes])
            thr = jnp.broadcast_to(through[b][:, h : h + 1], (1, HD))
            passed = passed * thr
            if b == 0:
                first_ref[lanes, :] = added
                thr_ref[h : h + 1, :] = thr
                state = added
            else:
                state = state * thr + added
        pay_ref[lanes, :] = state.astype(BF16)
        high = passed.astype(BF16)
        highs.append(high.astype(F32))
        lows.append(passed - high.astype(F32))
    none = jnp.zeros((8 - HEADS, HD), F32)
    pay_ref[HEADS * HD :, :] = jnp.concatenate(
        highs + [none] + lows + [none], axis=0
    ).astype(BF16)


def local_state(start, key_rows, values, keep_pad):
    tokens, width = key_rows.shape
    return pl.pallas_call(
        state_kernel,
        grid=(1,),
        in_specs=[smem(), whole((tokens, width)), whole((tokens, width)), whole((tokens, HD))],
        out_specs=[
            whole((width + 16, HD)),
            whole((width, HD)),
            whole((8, HD)),
            whole((tokens, HD)),
        ],
        out_shape=[
            jax.ShapeDtypeStruct((width + 16, HD), BF16),
            jax.ShapeDtypeStruct((width, HD), F32),
            jax.ShapeDtypeStruct((8, HD), F32),
            jax.ShapeDtypeStruct((tokens, HD), F32),
        ],
        compiler_params=pltpu.CompilerParams(vmem_limit_bytes=VMEM_LIMIT),
        cost_estimate=pl.CostEstimate(
            flops=2 * 10**9, bytes_accessed=4 * 10**6, transcendentals=10**5
        ),
        name="local_state",
    )(start, key_rows, values, keep_pad)


def intra_kernel(start_ref, q_ref, k_ref, v_ref, cum_ref, keep_t_ref, out_ref):
    start = start_ref[0]
    blocks = q_ref.shape[0] // BLK
    row = lax.broadcasted_iota(jnp.int32, (BLK, BLK), 0)
    col = lax.broadcasted_iota(jnp.int32, (BLK, BLK), 1)
    upper = (row <= col).astype(F32)
    part = BLK // 2
    for b in range(blocks):
        cum_t = jnp.dot(
            keep_t_ref[:, b * BLK : (b + 1) * BLK],
            upper,
            precision=HIGHEST,
            preferred_element_type=F32,
        )
        here = start - b * BLK
        for r in range(2):
            lo, n = r * part, (r + 1) * part
            t = lax.broadcasted_iota(jnp.int32, (part, n), 0) + lo
            s = lax.broadcasted_iota(jnp.int32, (part, n), 1)
            allowed = (t >= s) & ((s >= here) | (t < here))
            rows = pl.ds(b * BLK + lo, part)
            for h in range(HEADS):
                lanes = slice(h * HD, (h + 1) * HD)
                scores = lax.dot_general(
                    q_ref[rows, lanes],
                    k_ref[b * BLK : b * BLK + n, lanes],
                    (((1,), (1,)), ((), ())),
                    preferred_element_type=F32,
                )
                spread = cum_ref[rows, h : h + 1] - cum_t[h : h + 1, :n]
                decay = jnp.where(allowed, jnp.exp(jnp.where(allowed, spread, 0.0)), 0.0)
                weights = (scores * decay).astype(BF16)
                out_ref[rows, lanes] = jnp.dot(
                    weights, v_ref[b * BLK : b * BLK + n, lanes], preferred_element_type=F32
                )


def intra_part(start, queries, key_rows, values, cum, keep_t):
    tokens, width = queries.shape
    return pl.pallas_call(
        intra_kernel,
        grid=(1,),
        in_specs=[
            smem(),
            whole((tokens, width)),
            whole((tokens, width)),
            whole((tokens, width)),
            whole((tokens, HD)),
            whole((8, tokens)),
        ],
        out_specs=whole((tokens, width)),
        out_shape=jax.ShapeDtypeStruct((tokens, width), F32),
        compiler_params=pltpu.CompilerParams(vmem_limit_bytes=VMEM_LIMIT),
        cost_estimate=pl.CostEstimate(
            flops=8 * 10**9, bytes_accessed=6 * 10**6, transcendentals=2 * 10**6
        ),
        name="intra_part",
    )(start, queries, key_rows, values, cum, keep_t)


def passes_of(pay, h):
    base = HEADS * HD
    high = pay[base + h : base + h + 1, :].astype(F32)
    low = pay[base + 8 + h : base + 9 + h, :].astype(F32)
    return high + low


def row_kernel(place_ref, p0, p1, p2, p3, pay_ref, prefix_ref, through_ref):
    own = place_ref[0]
    parts = [p[...] for p in (p0, p1, p2, p3)]
    places = [lax.rem(own - d + GRID_SIDE, GRID_SIDE) for d in range(GRID_SIDE)]
    one = jnp.ones((1, HD), F32)
    through_ref[...] = jnp.zeros_like(through_ref)
    highs, lows = [], []
    for h in range(HEADS):
        lanes = slice(h * HD, (h + 1) * HD)
        thr = [passes_of(p, h) for p in parts]
        total = jnp.zeros((HD, HD), F32)
        prefix = jnp.zeros((HD, HD), F32)
        passed, before = one, one
        for d in range(GRID_SIDE):
            after, between = one, one
            for e in range(GRID_SIDE):
                if e == d:
                    continue
                later = places[e] > places[d]
                after = after * jnp.where(later, thr[e], one)
                between = between * jnp.where(later & (places[e] < own), thr[e], one)
            state = parts[d][lanes, :].astype(F32)
            total = total + state * after
            prefix = prefix + state * jnp.where(places[d] < own, between, 0.0 * one)
            passed = passed * thr[d]
            before = before * jnp.where(places[d] < own, thr[d], one)
        pay_ref[lanes, :] = total.astype(BF16)
        prefix_ref[lanes, :] = prefix
        through_ref[h : h + 1, :] = before
        high = passed.astype(BF16)
        highs.append(high.astype(F32))
        lows.append(passed - high.astype(F32))
    none = jnp.zeros((8 - HEADS, HD), F32)
    pay_ref[HEADS * HD :, :] = jnp.concatenate(
        highs + [none] + lows + [none], axis=0
    ).astype(BF16)


def row_states(place, parts):
    shape = parts[0].shape
    width = HEADS * HD
    return pl.pallas_call(
        row_kernel,
        grid=(1,),
        in_specs=[smem()] + [whole(shape)] * 4,
        out_specs=[whole(shape), whole((width, HD)), whole((8, HD))],
        out_shape=[
            jax.ShapeDtypeStruct(shape, BF16),
            jax.ShapeDtypeStruct((width, HD), F32),
            jax.ShapeDtypeStruct((8, HD), F32),
        ],
        cost_estimate=pl.CostEstimate(
            flops=10**6, bytes_accessed=10**6, transcendentals=0
        ),
        name="row_states",
    )(place, *parts)


def finish_kernel(
    start_ref, q_ref, intra_ref, cum_ref, e1, e2, e3, prefix_ref, before_ref, first_ref, thr_ref, *out_refs
):
    start = start_ref[0]
    blocks = q_ref.shape[0] // BLK
    rows1, rows2, rows3 = e1[...], e2[...], e3[...]
    place = lax.broadcasted_iota(jnp.int32, (BLK, HD), 0)
    factors = []
    for b in range(blocks):
        here = start - b * BLK
        opened = (place < here) | (here < 0)
        factors.append(jnp.where(opened, jnp.exp(cum_ref[pl.ds(b * BLK, BLK), :]), 0.0))
    for h in range(HEADS):
        lanes = slice(h * HD, (h + 1) * HD)
        far = rows2[lanes, :].astype(F32) + passes_of(rows2, h) * rows3[lanes, :].astype(F32)
        earlier = rows1[lanes, :].astype(F32) + passes_of(rows1, h) * far
        state = prefix_ref[lanes, :] + before_ref[h : h + 1, :] * earlier
        for b in range(blocks):
            own = pl.ds(b * BLK, BLK)
            if b > 0:
                state = state * thr_ref[h : h + 1, :] + first_ref[lanes, :]
            high = state.astype(BF16)
            low = (state - high.astype(F32)).astype(BF16)
            q = q_ref[own, lanes]
            carried = jnp.dot(q, high, preferred_element_type=F32) + jnp.dot(
                q, low, preferred_element_type=F32
            )
            heads = intra_ref[own, lanes] + carried * factors[b][:, h : h + 1]
            mean = jnp.mean(heads * heads, axis=1, keepdims=True)
            each = HEADS // 2
            half = slice(h % each * HD, (h % each + 1) * HD)
            out_refs[h // each][own, half] = (heads * lax.rsqrt(mean + EPSILON)).astype(BF16)


def finish(start, queries, intra, cum, rows, prefix, before, first, thr):
    tokens, width = queries.shape
    pay = rows[0].shape
    return pl.pallas_call(
        finish_kernel,
        grid=(1,),
        in_specs=[
            smem(),
            whole((tokens, width)),
            whole((tokens, width)),
            whole((tokens, HD)),
            whole(pay),
            whole(pay),
            whole(pay),
            whole((width, HD)),
            whole((8, HD)),
            whole((width, HD)),
            whole((8, HD)),
        ],
        out_specs=[whole((tokens, width // 2))] * 2,
        out_shape=[jax.ShapeDtypeStruct((tokens, width // 2), BF16)] * 2,
        compiler_params=pltpu.CompilerParams(vmem_limit_bytes=VMEM_LIMIT),
        cost_estimate=pl.CostEstimate(
            flops=10**9, bytes_accessed=5 * 10**6, transcendentals=10**6
        ),
        name="finish",
    )(start, queries, intra, cum, *rows, prefix, before, first, thr)


def proj_kernel(count, src_ref, *refs):
    xs = refs[:count]
    w_ref, res_ref, gain_ref, h_ref, x_ref = refs[count:]
    half = w_ref.shape[2]
    total = res_ref[...].astype(F32)
    for group in range(0, count, PROJ_GROUP):
        members = range(group, min(group + PROJ_GROUP, count))
        x = jnp.concatenate([xs[c][...] for c in members], axis=1)
        w = []
        for c in members:
            depth = xs[c].shape[1]
            at = pl.ds(pl.multiple_of(src_ref[c] * depth, depth), depth)
            w.append(jnp.concatenate([w_ref[0, at, :], w_ref[1, at, :]], axis=1))
        w = jnp.concatenate(w, axis=0)
        total = total + jnp.dot(x, w, preferred_element_type=F32)
    h_ref[...] = total.astype(BF16)
    rows = (total * gain_ref[...]).astype(BF16)
    x_ref[0] = rows[:, :half]
    x_ref[1] = rows[:, half:]


PROJ_GROUP = 4


def project(src, xs, weights, res, gain):
    tokens = xs[0].shape[0]
    part = weights.shape[2]
    columns = 2 * part
    tile = tokens // 2
    rows = lambda width: pl.BlockSpec((tile, width), lambda n, s: (n, 0))
    return pl.pallas_call(
        functools.partial(proj_kernel, len(xs)),
        grid_spec=pltpu.PrefetchScalarGridSpec(
            num_scalar_prefetch=1,
            grid=(tokens // tile,),
            in_specs=[rows(x.shape[1]) for x in xs]
            + [whole(weights.shape), rows(columns), whole((1, columns))],
            out_specs=[
                rows(columns),
                pl.BlockSpec((2, tile, part), lambda n, s: (0, n, 0)),
            ],
        ),
        out_shape=[
            jax.ShapeDtypeStruct((tokens, columns), BF16),
            jax.ShapeDtypeStruct((2, tokens, part), BF16),
        ],
        compiler_params=pltpu.CompilerParams(vmem_limit_bytes=VMEM_LIMIT),
        cost_estimate=pl.CostEstimate(
            flops=2 * tokens * columns * weights.shape[1],
            bytes_accessed=20 * 10**6,
            transcendentals=0,
        ),
        name="project",
    )(src, *xs, weights, res, gain)


NB = 128


def expert_kernel(count, begins, ends, src_ref, *refs):
    xs = refs[:count]
    gates = refs[count : 2 * count]
    ups = refs[2 * count : 3 * count]
    inverses = refs[3 * count : 4 * count]
    rest = refs[4 * count :]
    if not begins:
        sum_in, squares_in = rest[:2]
        rest = rest[2:]
    if ends:
        out_ref, squares_ref = rest
    else:
        sum_out, squares_ref = rest

    @pl.when(pl.program_id(0) == 0)
    def _():
        squares = None if begins else squares_in[...]
        for c in range(count):
            plain = xs[c][...].astype(F32) * inverses[c][...]
            plain = plain * plain
            for lane in range(plain.shape[1] // HD):
                part = plain[:, lane * HD : (lane + 1) * HD]
                squares = part if squares is None else squares + part
        if ends:
            mean = jnp.sum(squares, axis=1, keepdims=True) / ends
            squares = jnp.broadcast_to(lax.rsqrt(mean + EPSILON), squares.shape)
        squares_ref[...] = squares

    x = jnp.concatenate([xs[c][...] for c in range(count)], axis=1)
    w = [jnp.concatenate([gates[c][...], ups[c][...]], axis=1) for c in range(count)]
    total = jnp.dot(x, jnp.concatenate(w, axis=0), preferred_element_type=F32)
    if not begins:
        total = total + sum_in[0]
    if ends:
        scale = squares_ref[...]
        gate, up = total[:, :NB] * scale, total[:, NB:] * scale
        out_ref[...] = (gate / (1.0 + jnp.exp(-gate)) * up).astype(BF16)
    else:
        sum_out[0] = total


def expert_part(src, xs, gate_w, up_w, inverse, carried, ends=0, place=0):
    tokens = min(x.shape[0] for x in xs)
    hidden = gate_w.shape[1]
    w_specs, i_specs = [], []
    for c, x in enumerate(xs):
        depth = x.shape[1]
        w_specs.append(pl.BlockSpec((depth, NB), lambda n, s, c=c: (s[c], n)))
        i_specs.append(pl.BlockSpec((1, depth), lambda n, s, c=c: (0, s[c])))
    x_specs = [
        pl.BlockSpec(
            (tokens, x.shape[1]), lambda n, s, at=place if x.shape[0] > tokens else 0: (at, 0)
        )
        for x in xs
    ]
    kept = [
        pl.BlockSpec((1, tokens, 2 * NB), lambda n, s: (n, place, 0)),
        pl.BlockSpec((tokens, HD), lambda n, s: (place, 0)),
    ]
    if ends:
        out_specs = pl.BlockSpec((tokens, NB), lambda n, s: (0, n))
        out_shape = jax.ShapeDtypeStruct((tokens, hidden), BF16)
        scratch = [pltpu.VMEM((tokens, HD), F32)]
    else:
        out_specs = kept
        out_shape = [
            jax.ShapeDtypeStruct((hidden // NB, tokens, 2 * NB), F32),
            jax.ShapeDtypeStruct((tokens, HD), F32),
        ]
        scratch = []
    count = len(xs)
    return pl.pallas_call(
        functools.partial(expert_kernel, count, carried is None, ends),
        grid_spec=pltpu.PrefetchScalarGridSpec(
            num_scalar_prefetch=1,
            grid=(hidden // NB,),
            in_specs=x_specs
            + w_specs
            + w_specs
            + i_specs
            + ([] if carried is None else kept),
            out_specs=out_specs,
            scratch_shapes=scratch,
        ),
        out_shape=out_shape,
        compiler_params=pltpu.CompilerParams(vmem_limit_bytes=VMEM_LIMIT),
        cost_estimate=pl.CostEstimate(
            flops=4 * tokens * hidden * sum(x.shape[1] for x in xs),
            bytes_accessed=22 * 10**6,
            transcendentals=0,
        ),
        name="expert_part",
    )(
        src,
        *xs,
        *([gate_w] * count),
        *([up_w] * count),
        *([inverse] * count),
        *(() if carried is None else carried),
    )


def moved(block, axis, place_to):
    count = lax.axis_size(axis)
    return lax.ppermute(block, axis, [(i, place_to(i)) for i in range(count)])


def along(block, steps, cross=0):
    count = lax.axis_size("expert")
    return moved(block, "expert", lambda j: ((j // 2 + steps) * 2 + (j % 2 ^ cross)) % count)


class Ring:
    def __init__(self, me):
        self.count = lax.axis_size("expert")
        self.me, self.other = me, me + 1 - 2 * lax.rem(me, 2)

    def named(self, block, owner, steps, half):
        return block, 2 * lax.rem(owner + 2 * steps + self.count, self.count) + half

    def near(self, block, half):
        return (
            [self.named(block, self.me, 0, half), self.named(along(block, 0, 1), self.other, 0, half)],
            along(block, 1),
            along(block, -1),
        )

    def shared(self, below, above, half):
        return [
            self.both(below, -1, half),
            self.both(above, 1, half),
        ]

    def far(self, below, above, half):
        return self.both(along(above, -1) if half else along(below, 1), 2, half)

    def both(self, block, steps, half):
        return [
            self.named(block, self.me, steps, half),
            self.named(along(block, 0, 1), self.other, steps, half),
        ]


def returned(block, me):
    count = lax.axis_size("expert")
    rows = block.shape[0] // count
    parts = []
    for steps in range(count // 2):
        for cross in range(2):
            across = (1 - 2 * lax.rem(me, 2)) * cross
            to = lax.rem(me + across + 2 * steps, count)
            part = lax.dynamic_slice_in_dim(block, to * rows, rows, 0)
            if steps or cross:
                part = along(part, steps, cross)
            parts.append((part, lax.rem(me + across - 2 * steps + count, count)))
    return parts


def unzip(pairs):
    return [x for x, _ in pairs], jnp.stack([s for _, s in pairs]).astype(jnp.int32)


def on_device(
    residual_in,
    queries,
    key_rows,
    values,
    log_keep,
    prompt_start,
    out_proj,
    norm_gain,
    expert_ids,
    w_gate,
    w_up,
):
    tok_rows, model_width = residual_in.shape
    section_len = queries.shape[0]
    span_count = lax.axis_size("span")
    slice_count = lax.axis_size("expert")
    capacity = max(2, tok_rows * 5 // (4 * span_count))
    my_span = lax.axis_index("span")
    my_slice = lax.axis_index("expert")
    columns = model_width // slice_count

    pairs = []
    for i in range(span_count):
        for j in range(slice_count):
            pairs.append((i * slice_count + j, (i % 2 * slice_count + j) * slice_count + i // 2))
    piece = lax.ppermute(out_proj, ("span", "expert"), pairs)

    keep_pad = jnp.pad(log_keep, ((0, 0), (0, HD - log_keep.shape[1])))
    keep_t = jnp.pad(log_keep.T, ((0, 8 - log_keep.shape[1]), (0, 0)))
    pay, first, thr, cum = local_state(prompt_start, key_rows, values, keep_pad)
    side = GRID_SIDE
    in_row = [
        moved(pay, "span", lambda i, d=d: i // side * side + (i + d) % side)
        for d in range(1, side)
    ]
    piece, residual, *in_row = lax.optimization_barrier((piece, residual_in, *in_row))
    proj_w = lax.all_gather(piece, "span", axis=0)
    proj_w = proj_w.reshape(2, slice_count * out_proj.shape[0], out_proj.shape[1])
    named = jnp.broadcast_to(expert_ids.astype(BF16)[:, :, None], (tok_rows, slice_count, HD))
    res = jnp.concatenate([residual.reshape(tok_rows, slice_count, columns), named], axis=2)
    res = lax.all_to_all(res, "expert", split_axis=1, concat_axis=0, tiled=True)
    res = res.reshape(section_len, columns + HD)
    intra = intra_part(prompt_start, queries, key_rows, values, cum, keep_t)
    place = lax.rem(my_span, side)[None].astype(jnp.int32)
    row_pay, prefix, before = row_states(place, [pay] + in_row)
    rows = [
        lax.ppermute(
            row_pay,
            "span",
            [(i, i + d * side) for i in range(span_count) if i + d * side < span_count],
        )
        for d in range(1, side)
    ]
    normed = finish(prompt_start, queries, intra, cum, rows, prefix, before, first, thr)

    res, *normed = lax.optimization_barrier((res, *normed))
    ids = res[:, columns].astype(jnp.int32).reshape(slice_count, tok_rows)
    onehot = (ids[:, :, None] == jnp.arange(span_count)[None, None, :]).astype(BF16)
    earlier = jnp.tril(jnp.ones((tok_rows, tok_rows), BF16), -1)
    earlier_count = jnp.einsum("ts,bse->bte", earlier, onehot, preferred_element_type=F32)
    slot = jnp.sum(earlier_count * onehot.astype(F32), axis=2).astype(jnp.int32)
    block_of = jnp.arange(slice_count)[:, None]
    target = ((ids * slice_count + block_of) * capacity + slot).reshape(-1)
    slots = span_count * slice_count * capacity
    placing = (jnp.arange(slots)[:, None] == target[None, :]).astype(BF16)
    r = jnp.arange(slots)
    block, inner = r // (span_count * capacity), r % (span_count * capacity)
    wanted = (inner // capacity * slice_count + block) * capacity + inner % capacity
    turning = (wanted[:, None] == r[None, :]).astype(BF16)

    ring = Ring(my_slice)
    chunks, kept = [], []
    for half in range(2):
        own, below, above = ring.near(normed[half], half)
        chunks += own
        kept.append((below, above))
    for half in range(2):
        chunks += ring.far(*kept[half], half)
        chunks += sum(ring.shared(*kept[half], half), [])
    xs, src = unzip(chunks)
    gain_cols = lax.dynamic_slice_in_dim(norm_gain, my_slice * columns, columns)[None, :]
    hidden_cols, rows_in = project(src, xs, proj_w, res, gain_cols)
    hidden_parts = returned(hidden_cols, my_slice)
    first_rows, second_rows = rows_in[0], rows_in[1]

    def packed(rows):
        chosen = jnp.dot(placing, rows, preferred_element_type=F32).astype(BF16)
        return chosen.reshape(span_count, slice_count * capacity, columns // 2)

    def dispatched(rows):
        arrived = lax.all_to_all(rows, "span", split_axis=0, concat_axis=0, tiled=True)
        return arrived.reshape(slots, columns // 2)

    inverse = (1.0 / norm_gain)[None, :]
    gate_w, up_w = w_gate[0], w_up[0]

    def expert(group, carried, ends=0, place=0):
        xs, src = unzip(group)
        return expert_part(src, xs, gate_w, up_w, inverse, carried, ends, place)

    arrived_a = dispatched(packed(first_rows))
    own_a, below_a, above_a = ring.near(arrived_a, 0)
    packed_b, hidden_parts = lax.optimization_barrier((packed(second_rows), hidden_parts))
    arrived_b = dispatched(packed_b)
    arrived_b, below_a, above_a = lax.optimization_barrier((arrived_b, below_a, above_a))
    own_b, below_b, above_b = ring.near(arrived_b, 1)
    (from_below, from_below_other), (from_above, from_above_other) = ring.shared(below_a, above_a, 0)
    far_a = ring.far(below_a, above_a, 0)
    carried = expert(own_a + [from_below, from_above], None)
    carried = expert(own_b + [from_below_other, from_above_other], carried)
    carried, above_b = lax.optimization_barrier((carried, above_b))
    cut = slots // 2
    tails = [along(above_b[at:at + cut], -1) for at in (0, cut)]
    carried = expert(sum(ring.shared(below_b, above_b, 1), []), carried)
    carried, *tails = lax.optimization_barrier((carried, *tails))
    far_b = [ring.both(tail, 2, 1) for tail in tails]
    first_half = expert(far_a + far_b[0], carried, model_width, 0)
    hidden_rows = jnp.dot(turning[:, :cut], first_half, preferred_element_type=F32)
    second_half = expert(far_a + far_b[1], carried, model_width, 1)
    hidden_rows = hidden_rows.astype(BF16).astype(F32) + jnp.dot(
        turning[:, cut:], second_half, preferred_element_type=F32
    )
    hidden_rows = hidden_rows.astype(BF16)
    hidden_state = jnp.zeros((tok_rows, model_width), BF16)
    for part, owner in hidden_parts:
        hidden_state = lax.dynamic_update_slice_in_dim(hidden_state, part, owner * columns, 1)
    return (hidden_state, hidden_rows[None])


def solution(mesh):
    placed = (
        P(("span", "expert"), None),
        P("span", "expert"),
        P("span", "expert"),
        P("span", "expert"),
        P("span", "expert"),
        P("span"),
        P("expert", "span"),
        P(),
        P(("span", "expert"), None),
        P("span", None, "expert"),
        P("span", None, "expert"),
    )
    return jax.shard_map(
        on_device,
        mesh=mesh,
        in_specs=placed,
        out_specs=(P(("span", "expert"), None), P("span", None, "expert")),
        check_vma=False,
    )
```

```python
import functools

import jax
import jax.numpy as jnp
from jax import lax
from jax.experimental import pallas as pl
from jax.experimental.pallas import tpu as pltpu
from jax.sharding import PartitionSpec as P

BLK = 512
EPSILON = 1e-05
HIGHEST = lax.Precision.HIGHEST
F32 = jnp.float32
BF16 = jnp.bfloat16
VMEM_LIMIT = 56 * 1024 * 1024
HEADS = 4
HD = 128
GRID_SIDE = 4


def whole(shape):
    return pl.BlockSpec(shape, lambda *_: (0,) * len(shape))


def smem():
    return pl.BlockSpec(memory_space=pltpu.SMEM)


def split_dot(a_f32, b_bf16):
    high = a_f32.astype(BF16)
    low = (a_f32 - high.astype(F32)).astype(BF16)
    return jnp.dot(high, b_bf16, preferred_element_type=F32) + jnp.dot(
        low, b_bf16, preferred_element_type=F32
    )


def state_kernel(start_ref, k_ref, v_ref, keep_ref, pay_ref, first_ref, thr_ref, cum_ref):
    start = start_ref[0]
    blocks = k_ref.shape[0] // BLK
    row = lax.broadcasted_iota(jnp.int32, (BLK, BLK), 0)
    col = lax.broadcasted_iota(jnp.int32, (BLK, BLK), 1)
    lower = (row >= col).astype(F32)
    place = lax.broadcasted_iota(jnp.int32, (BLK, HD), 0)
    through, tails = [], []
    for b in range(blocks):
        own = pl.ds(b * BLK, BLK)
        cum = jnp.dot(lower, keep_ref[own, :], precision=HIGHEST, preferred_element_type=F32)
        cum_ref[own, :] = cum
        end = cum[BLK - 1 :, :]
        here = start - b * BLK
        same = (place >= here) == (here <= BLK - 1)
        tails.append(jnp.where(same, jnp.exp(end - cum), 0.0))
        resets = (here >= 0) & (here < BLK)
        through.append(jnp.where(resets, 0.0, jnp.exp(end)))
    pay_ref[HEADS * HD :, :] = jnp.zeros_like(pay_ref[HEADS * HD :, :])
    thr_ref[...] = jnp.zeros_like(thr_ref)
    highs, lows = [], []
    for h in range(HEADS):
        lanes = slice(h * HD, (h + 1) * HD)
        state = None
        passed = jnp.ones((1, HD), F32)
        for b in range(blocks):
            own = pl.ds(b * BLK, BLK)
            key = k_ref[own, lanes].astype(F32) * tails[b][:, h : h + 1]
            added = split_dot(key.T, v_ref[own, lanes])
            thr = jnp.broadcast_to(through[b][:, h : h + 1], (1, HD))
            passed = passed * thr
            if b == 0:
                first_ref[lanes, :] = added
                thr_ref[h : h + 1, :] = thr
                state = added
            else:
                state = state * thr + added
        pay_ref[lanes, :] = state.astype(BF16)
        high = passed.astype(BF16)
        highs.append(high.astype(F32))
        lows.append(passed - high.astype(F32))
    none = jnp.zeros((8 - HEADS, HD), F32)
    pay_ref[HEADS * HD :, :] = jnp.concatenate(
        highs + [none] + lows + [none], axis=0
    ).astype(BF16)


def local_state(start, key_rows, values, keep_pad):
    tokens, width = key_rows.shape
    return pl.pallas_call(
        state_kernel,
        grid=(1,),
        in_specs=[smem(), whole((tokens, width)), whole((tokens, width)), whole((tokens, HD))],
        out_specs=[
            whole((width + 16, HD)),
            whole((width, HD)),
            whole((8, HD)),
            whole((tokens, HD)),
        ],
        out_shape=[
            jax.ShapeDtypeStruct((width + 16, HD), BF16),
            jax.ShapeDtypeStruct((width, HD), F32),
            jax.ShapeDtypeStruct((8, HD), F32),
            jax.ShapeDtypeStruct((tokens, HD), F32),
        ],
        compiler_params=pltpu.CompilerParams(vmem_limit_bytes=VMEM_LIMIT),
        cost_estimate=pl.CostEstimate(
            flops=2 * 10**9, bytes_accessed=4 * 10**6, transcendentals=10**5
        ),
        name="local_state",
    )(start, key_rows, values, keep_pad)


def intra_kernel(start_ref, q_ref, k_ref, v_ref, cum_ref, keep_t_ref, out_ref):
    start = start_ref[0]
    blocks = q_ref.shape[0] // BLK
    row = lax.broadcasted_iota(jnp.int32, (BLK, BLK), 0)
    col = lax.broadcasted_iota(jnp.int32, (BLK, BLK), 1)
    upper = (row <= col).astype(F32)
    part = BLK // 2
    for b in range(blocks):
        cum_t = jnp.dot(
            keep_t_ref[:, b * BLK : (b + 1) * BLK],
            upper,
            precision=HIGHEST,
            preferred_element_type=F32,
        )
        here = start - b * BLK
        for r in range(2):
            lo, n = r * part, (r + 1) * part
            t = lax.broadcasted_iota(jnp.int32, (part, n), 0) + lo
            s = lax.broadcasted_iota(jnp.int32, (part, n), 1)
            allowed = (t >= s) & ((s >= here) | (t < here))
            rows = pl.ds(b * BLK + lo, part)
            for h in range(HEADS):
                lanes = slice(h * HD, (h + 1) * HD)
                scores = lax.dot_general(
                    q_ref[rows, lanes],
                    k_ref[b * BLK : b * BLK + n, lanes],
                    (((1,), (1,)), ((), ())),
                    preferred_element_type=F32,
                )
                spread = cum_ref[rows, h : h + 1] - cum_t[h : h + 1, :n]
                decay = jnp.where(allowed, jnp.exp(jnp.where(allowed, spread, 0.0)), 0.0)
                weights = (scores * decay).astype(BF16)
                out_ref[rows, lanes] = jnp.dot(
                    weights, v_ref[b * BLK : b * BLK + n, lanes], preferred_element_type=F32
                )


def intra_part(start, queries, key_rows, values, cum, keep_t):
    tokens, width = queries.shape
    return pl.pallas_call(
        intra_kernel,
        grid=(1,),
        in_specs=[
            smem(),
            whole((tokens, width)),
            whole((tokens, width)),
            whole((tokens, width)),
            whole((tokens, HD)),
            whole((8, tokens)),
        ],
        out_specs=whole((tokens, width)),
        out_shape=jax.ShapeDtypeStruct((tokens, width), F32),
        compiler_params=pltpu.CompilerParams(vmem_limit_bytes=VMEM_LIMIT),
        cost_estimate=pl.CostEstimate(
            flops=8 * 10**9, bytes_accessed=6 * 10**6, transcendentals=2 * 10**6
        ),
        name="intra_part",
    )(start, queries, key_rows, values, cum, keep_t)


def passes_of(pay, h):
    base = HEADS * HD
    high = pay[base + h : base + h + 1, :].astype(F32)
    low = pay[base + 8 + h : base + 9 + h, :].astype(F32)
    return high + low


def row_kernel(place_ref, p0, p1, p2, p3, pay_ref, prefix_ref, through_ref):
    own = place_ref[0]
    parts = [p[...] for p in (p0, p1, p2, p3)]
    places = [lax.rem(own - d + GRID_SIDE, GRID_SIDE) for d in range(GRID_SIDE)]
    one = jnp.ones((1, HD), F32)
    through_ref[...] = jnp.zeros_like(through_ref)
    highs, lows = [], []
    for h in range(HEADS):
        lanes = slice(h * HD, (h + 1) * HD)
        thr = [passes_of(p, h) for p in parts]
        total = jnp.zeros((HD, HD), F32)
        prefix = jnp.zeros((HD, HD), F32)
        passed, before = one, one
        for d in range(GRID_SIDE):
            after, between = one, one
            for e in range(GRID_SIDE):
                if e == d:
                    continue
                later = places[e] > places[d]
                after = after * jnp.where(later, thr[e], one)
                between = between * jnp.where(later & (places[e] < own), thr[e], one)
            state = parts[d][lanes, :].astype(F32)
            total = total + state * after
            prefix = prefix + state * jnp.where(places[d] < own, between, 0.0 * one)
            passed = passed * thr[d]
            before = before * jnp.where(places[d] < own, thr[d], one)
        pay_ref[lanes, :] = total.astype(BF16)
        prefix_ref[lanes, :] = prefix
        through_ref[h : h + 1, :] = before
        high = passed.astype(BF16)
        highs.append(high.astype(F32))
        lows.append(passed - high.astype(F32))
    none = jnp.zeros((8 - HEADS, HD), F32)
    pay_ref[HEADS * HD :, :] = jnp.concatenate(
        highs + [none] + lows + [none], axis=0
    ).astype(BF16)


def row_states(place, parts):
    shape = parts[0].shape
    width = HEADS * HD
    return pl.pallas_call(
        row_kernel,
        grid=(1,),
        in_specs=[smem()] + [whole(shape)] * 4,
        out_specs=[whole(shape), whole((width, HD)), whole((8, HD))],
        out_shape=[
            jax.ShapeDtypeStruct(shape, BF16),
            jax.ShapeDtypeStruct((width, HD), F32),
            jax.ShapeDtypeStruct((8, HD), F32),
        ],
        cost_estimate=pl.CostEstimate(
            flops=10**6, bytes_accessed=10**6, transcendentals=0
        ),
        name="row_states",
    )(place, *parts)


def finish_kernel(
    start_ref, q_ref, intra_ref, cum_ref, e1, e2, e3, prefix_ref, before_ref, first_ref, thr_ref, *out_refs
):
    start = start_ref[0]
    blocks = q_ref.shape[0] // BLK
    rows1, rows2, rows3 = e1[...], e2[...], e3[...]
    place = lax.broadcasted_iota(jnp.int32, (BLK, HD), 0)
    factors = []
    for b in range(blocks):
        here = start - b * BLK
        opened = (place < here) | (here < 0)
        factors.append(jnp.where(opened, jnp.exp(cum_ref[pl.ds(b * BLK, BLK), :]), 0.0))
    for h in range(HEADS):
        lanes = slice(h * HD, (h + 1) * HD)
        far = rows2[lanes, :].astype(F32) + passes_of(rows2, h) * rows3[lanes, :].astype(F32)
        earlier = rows1[lanes, :].astype(F32) + passes_of(rows1, h) * far
        state = prefix_ref[lanes, :] + before_ref[h : h + 1, :] * earlier
        for b in range(blocks):
            own = pl.ds(b * BLK, BLK)
            if b > 0:
                state = state * thr_ref[h : h + 1, :] + first_ref[lanes, :]
            high = state.astype(BF16)
            low = (state - high.astype(F32)).astype(BF16)
            q = q_ref[own, lanes]
            carried = jnp.dot(q, high, preferred_element_type=F32) + jnp.dot(
                q, low, preferred_element_type=F32
            )
            heads = intra_ref[own, lanes] + carried * factors[b][:, h : h + 1]
            mean = jnp.mean(heads * heads, axis=1, keepdims=True)
            each = HEADS // 2
            half = slice(h % each * HD, (h % each + 1) * HD)
            out_refs[h // each][own, half] = (heads * lax.rsqrt(mean + EPSILON)).astype(BF16)


def finish(start, queries, intra, cum, rows, prefix, before, first, thr):
    tokens, width = queries.shape
    pay = rows[0].shape
    return pl.pallas_call(
        finish_kernel,
        grid=(1,),
        in_specs=[
            smem(),
            whole((tokens, width)),
            whole((tokens, width)),
            whole((tokens, HD)),
            whole(pay),
            whole(pay),
            whole(pay),
            whole((width, HD)),
            whole((8, HD)),
            whole((width, HD)),
            whole((8, HD)),
        ],
        out_specs=[whole((tokens, width // 2))] * 2,
        out_shape=[jax.ShapeDtypeStruct((tokens, width // 2), BF16)] * 2,
        compiler_params=pltpu.CompilerParams(vmem_limit_bytes=VMEM_LIMIT),
        cost_estimate=pl.CostEstimate(
            flops=10**9, bytes_accessed=5 * 10**6, transcendentals=10**6
        ),
        name="finish",
    )(start, queries, intra, cum, *rows, prefix, before, first, thr)


def proj_kernel(count, src_ref, *refs):
    xs = refs[:count]
    w_ref, res_ref, gain_ref, h_ref, x_ref = refs[count:]
    half = w_ref.shape[2]
    total = res_ref[...].astype(F32)
    for group in range(0, count, PROJ_GROUP):
        members = range(group, min(group + PROJ_GROUP, count))
        x = jnp.concatenate([xs[c][...] for c in members], axis=1)
        w = []
        for c in members:
            depth = xs[c].shape[1]
            at = pl.ds(pl.multiple_of(src_ref[c] * depth, depth), depth)
            w.append(jnp.concatenate([w_ref[0, at, :], w_ref[1, at, :]], axis=1))
        w = jnp.concatenate(w, axis=0)
        total = total + jnp.dot(x, w, preferred_element_type=F32)
    h_ref[...] = total.astype(BF16)
    rows = (total * gain_ref[...]).astype(BF16)
    x_ref[0] = rows[:, :half]
    x_ref[1] = rows[:, half:]


PROJ_GROUP = 4


def project(src, xs, weights, res, gain):
    tokens = xs[0].shape[0]
    part = weights.shape[2]
    columns = 2 * part
    tile = tokens // 2
    rows = lambda width: pl.BlockSpec((tile, width), lambda n, s: (n, 0))
    return pl.pallas_call(
        functools.partial(proj_kernel, len(xs)),
        grid_spec=pltpu.PrefetchScalarGridSpec(
            num_scalar_prefetch=1,
            grid=(tokens // tile,),
            in_specs=[rows(x.shape[1]) for x in xs]
            + [whole(weights.shape), rows(columns), whole((1, columns))],
            out_specs=[
                rows(columns),
                pl.BlockSpec((2, tile, part), lambda n, s: (0, n, 0)),
            ],
        ),
        out_shape=[
            jax.ShapeDtypeStruct((tokens, columns), BF16),
            jax.ShapeDtypeStruct((2, tokens, part), BF16),
        ],
        compiler_params=pltpu.CompilerParams(vmem_limit_bytes=VMEM_LIMIT),
        cost_estimate=pl.CostEstimate(
            flops=2 * tokens * columns * weights.shape[1],
            bytes_accessed=20 * 10**6,
            transcendentals=0,
        ),
        name="project",
    )(src, *xs, weights, res, gain)


NB = 128


def expert_kernel(count, begins, ends, steps, src_ref, *refs):
    xs = refs[:count]
    gates = refs[count : 2 * count]
    ups = refs[2 * count : 3 * count]
    inverses = refs[3 * count : 4 * count]
    rest = refs[4 * count :]
    if not begins:
        sum_in, squares_in = rest[:2]
        rest = rest[2:]
    if ends:
        out_ref, squares_ref = rest
    else:
        sum_out, squares_ref = rest

    def squared(rows):
        squares = None if begins else squares_in[rows, :]
        for c in range(count):
            plain = xs[c][rows, :].astype(F32) * inverses[c][...]
            plain = plain * plain
            for lane in range(plain.shape[1] // HD):
                part = plain[:, lane * HD : (lane + 1) * HD]
                squares = part if squares is None else squares + part
        return squares

    if ends:

        @pl.when(pl.program_id(0) == 0)
        def _():
            squares = squared(slice(None))
            mean = jnp.sum(squares, axis=1, keepdims=True) / ends
            squares_ref[...] = jnp.broadcast_to(lax.rsqrt(mean + EPSILON), squares.shape)

    else:
        share = xs[0].shape[0] // steps
        at = pl.ds(pl.multiple_of(pl.program_id(0) * share, share), share)
        squares_ref[at, :] = squared(at)

    x = jnp.concatenate([xs[c][...] for c in range(count)], axis=1)
    w = [jnp.concatenate([gates[c][...], ups[c][...]], axis=1) for c in range(count)]
    total = jnp.dot(x, jnp.concatenate(w, axis=0), preferred_element_type=F32)
    if not begins:
        total = total + sum_in[0]
    if ends:
        scale = squares_ref[...]
        gate, up = total[:, :NB] * scale, total[:, NB:] * scale
        out_ref[...] = (gate / (1.0 + jnp.exp(-gate)) * up).astype(BF16)
    else:
        sum_out[0] = total


def expert_part(src, xs, gate_w, up_w, inverse, carried, ends=0, place=0):
    tokens = min(x.shape[0] for x in xs)
    hidden = gate_w.shape[1]
    w_specs, i_specs = [], []
    for c, x in enumerate(xs):
        depth = x.shape[1]
        w_specs.append(pl.BlockSpec((depth, NB), lambda n, s, c=c: (s[c], n)))
        i_specs.append(pl.BlockSpec((1, depth), lambda n, s, c=c: (0, s[c])))
    x_specs = [
        pl.BlockSpec(
            (tokens, x.shape[1]), lambda n, s, at=place if x.shape[0] > tokens else 0: (at, 0)
        )
        for x in xs
    ]
    kept = [
        pl.BlockSpec((1, tokens, 2 * NB), lambda n, s: (n, place, 0)),
        pl.BlockSpec((tokens, HD), lambda n, s: (place, 0)),
    ]
    if ends:
        out_specs = pl.BlockSpec((tokens, NB), lambda n, s: (0, n))
        out_shape = jax.ShapeDtypeStruct((tokens, hidden), BF16)
        scratch = [pltpu.VMEM((tokens, HD), F32)]
    else:
        out_specs = kept
        out_shape = [
            jax.ShapeDtypeStruct((hidden // NB, tokens, 2 * NB), F32),
            jax.ShapeDtypeStruct((tokens, HD), F32),
        ]
        scratch = []
    count = len(xs)
    return pl.pallas_call(
        functools.partial(expert_kernel, count, carried is None, ends, hidden // NB),
        grid_spec=pltpu.PrefetchScalarGridSpec(
            num_scalar_prefetch=1,
            grid=(hidden // NB,),
            in_specs=x_specs
            + w_specs
            + w_specs
            + i_specs
            + ([] if carried is None else kept),
            out_specs=out_specs,
            scratch_shapes=scratch,
        ),
        out_shape=out_shape,
        compiler_params=pltpu.CompilerParams(vmem_limit_bytes=VMEM_LIMIT),
        cost_estimate=pl.CostEstimate(
            flops=4 * tokens * hidden * sum(x.shape[1] for x in xs),
            bytes_accessed=22 * 10**6,
            transcendentals=0,
        ),
        name="expert_part",
    )(
        src,
        *xs,
        *([gate_w] * count),
        *([up_w] * count),
        *([inverse] * count),
        *(() if carried is None else carried),
    )


def assemble_kernel(count, src_ref, *refs):
    out_ref = refs[count]
    for c in range(count):
        width = refs[c].shape[1]
        at = pl.ds(pl.multiple_of(src_ref[c] * width, width), width)
        out_ref[:, at] = refs[c][...]


def assembled(pairs, columns):
    parts, src = unzip(pairs)
    count = len(parts)
    rows = parts[0].shape[0]
    return pl.pallas_call(
        functools.partial(assemble_kernel, count),
        grid_spec=pltpu.PrefetchScalarGridSpec(
            num_scalar_prefetch=1,
            grid=(1,),
            in_specs=[whole(p.shape) for p in parts],
            out_specs=whole((rows, count * columns)),
        ),
        out_shape=jax.ShapeDtypeStruct((rows, count * columns), BF16),
        cost_estimate=pl.CostEstimate(
            flops=0, bytes_accessed=4 * rows * count * columns, transcendentals=0
        ),
        name="assembled",
    )(src, *parts)


def moved(block, axis, place_to):
    count = lax.axis_size(axis)
    return lax.ppermute(block, axis, [(i, place_to(i)) for i in range(count)])


def along(block, steps, cross=0):
    count = lax.axis_size("expert")
    return moved(block, "expert", lambda j: ((j // 2 + steps) * 2 + (j % 2 ^ cross)) % count)


class Ring:
    def __init__(self, me):
        self.count = lax.axis_size("expert")
        self.me, self.other = me, me + 1 - 2 * lax.rem(me, 2)

    def named(self, block, owner, steps, half):
        return block, 2 * lax.rem(owner + 2 * steps + self.count, self.count) + half

    def near(self, block, half):
        return (
            [self.named(block, self.me, 0, half), self.named(along(block, 0, 1), self.other, 0, half)],
            along(block, 1),
            along(block, -1),
        )

    def shared(self, below, above, half):
        return [
            self.both(below, -1, half),
            self.both(above, 1, half),
        ]

    def far(self, below, above, half):
        return self.both(along(above, -1) if half else along(below, 1), 2, half)

    def both(self, block, steps, half):
        return [
            self.named(block, self.me, steps, half),
            self.named(along(block, 0, 1), self.other, steps, half),
        ]


def returned(block, me):
    count = lax.axis_size("expert")
    rows = block.shape[0] // count
    parts = []
    for steps in range(count // 2):
        for cross in range(2):
            across = (1 - 2 * lax.rem(me, 2)) * cross
            to = lax.rem(me + across + 2 * steps, count)
            part = lax.dynamic_slice_in_dim(block, to * rows, rows, 0)
            if steps or cross:
                part = along(part, steps, cross)
            parts.append((part, lax.rem(me + across - 2 * steps + count, count)))
    return parts


def unzip(pairs):
    return [x for x, _ in pairs], jnp.stack([s for _, s in pairs]).astype(jnp.int32)


def on_device(
    residual_in,
    queries,
    key_rows,
    values,
    log_keep,
    prompt_start,
    out_proj,
    norm_gain,
    expert_ids,
    w_gate,
    w_up,
):
    tok_rows, model_width = residual_in.shape
    section_len = queries.shape[0]
    span_count = lax.axis_size("span")
    slice_count = lax.axis_size("expert")
    capacity = max(2, tok_rows * 5 // (4 * span_count))
    my_span = lax.axis_index("span")
    my_slice = lax.axis_index("expert")
    columns = model_width // slice_count

    pairs = []
    for i in range(span_count):
        for j in range(slice_count):
            pairs.append((i * slice_count + j, (i % 2 * slice_count + j) * slice_count + i // 2))
    piece = lax.ppermute(out_proj, ("span", "expert"), pairs)

    keep_pad = jnp.pad(log_keep, ((0, 0), (0, HD - log_keep.shape[1])))
    keep_t = jnp.pad(log_keep.T, ((0, 8 - log_keep.shape[1]), (0, 0)))
    pay, first, thr, cum = local_state(prompt_start, key_rows, values, keep_pad)
    side = GRID_SIDE
    in_row = [
        moved(pay, "span", lambda i, d=d: i // side * side + (i + d) % side)
        for d in range(1, side)
    ]
    piece, residual, *in_row = lax.optimization_barrier((piece, residual_in, *in_row))
    proj_w = lax.all_gather(piece, "span", axis=0)
    proj_w = proj_w.reshape(2, slice_count * out_proj.shape[0], out_proj.shape[1])
    named = jnp.broadcast_to(expert_ids.astype(BF16)[:, :, None], (tok_rows, slice_count, HD))
    res = jnp.concatenate([residual.reshape(tok_rows, slice_count, columns), named], axis=2)
    res = lax.all_to_all(res, "expert", split_axis=1, concat_axis=0, tiled=True)
    res = res.reshape(section_len, columns + HD)
    intra = intra_part(prompt_start, queries, key_rows, values, cum, keep_t)
    place = lax.rem(my_span, side)[None].astype(jnp.int32)
    row_pay, prefix, before = row_states(place, [pay] + in_row)
    rows = [
        lax.ppermute(
            row_pay,
            "span",
            [(i, i + d * side) for i in range(span_count) if i + d * side < span_count],
        )
        for d in range(1, side)
    ]
    normed = finish(prompt_start, queries, intra, cum, rows, prefix, before, first, thr)

    res, *normed = lax.optimization_barrier((res, *normed))
    ids = res[:, columns].astype(jnp.int32).reshape(slice_count, tok_rows)
    onehot = (ids[:, :, None] == jnp.arange(span_count)[None, None, :]).astype(BF16)
    earlier = jnp.tril(jnp.ones((tok_rows, tok_rows), BF16), -1)
    earlier_count = jnp.einsum("ts,bse->bte", earlier, onehot, preferred_element_type=F32)
    slot = jnp.sum(earlier_count * onehot.astype(F32), axis=2).astype(jnp.int32)
    block_of = jnp.arange(slice_count)[:, None]
    target = ((ids * slice_count + block_of) * capacity + slot).reshape(-1)
    slots = span_count * slice_count * capacity
    placing = (jnp.arange(slots)[:, None] == target[None, :]).astype(BF16)
    r = jnp.arange(slots)
    block, inner = r // (span_count * capacity), r % (span_count * capacity)
    wanted = (inner // capacity * slice_count + block) * capacity + inner % capacity
    turning = (wanted[:, None] == r[None, :]).astype(BF16)

    ring = Ring(my_slice)
    chunks, kept = [], []
    for half in range(2):
        own, below, above = ring.near(normed[half], half)
        chunks += own
        kept.append((below, above))
    for half in range(2):
        chunks += ring.far(*kept[half], half)
        chunks += sum(ring.shared(*kept[half], half), [])
    xs, src = unzip(chunks)
    gain_cols = lax.dynamic_slice_in_dim(norm_gain, my_slice * columns, columns)[None, :]
    hidden_cols, rows_in = project(src, xs, proj_w, res, gain_cols)
    hidden_parts = returned(hidden_cols, my_slice)
    first_rows, second_rows = rows_in[0], rows_in[1]

    def packed(rows):
        chosen = jnp.dot(placing, rows, preferred_element_type=F32).astype(BF16)
        return chosen.reshape(span_count, slice_count * capacity, columns // 2)

    def dispatched(rows):
        arrived = lax.all_to_all(rows, "span", split_axis=0, concat_axis=0, tiled=True)
        return arrived.reshape(slots, columns // 2)

    inverse = (1.0 / norm_gain)[None, :]
    gate_w, up_w = w_gate[0], w_up[0]

    def expert(group, carried, ends=0, place=0):
        xs, src = unzip(group)
        return expert_part(src, xs, gate_w, up_w, inverse, carried, ends, place)

    arrived_a, packed_b = lax.optimization_barrier(
        (dispatched(packed(first_rows)), packed(second_rows))
    )
    own_a, below_a, above_a = ring.near(arrived_a, 0)
    packed_b, hidden_parts = lax.optimization_barrier((packed_b, hidden_parts))
    arrived_b = dispatched(packed_b)
    arrived_b, below_a, above_a = lax.optimization_barrier((arrived_b, below_a, above_a))
    own_b, below_b, above_b = ring.near(arrived_b, 1)
    (from_below, from_below_other), (from_above, from_above_other) = ring.shared(below_a, above_a, 0)
    carried = expert(own_a + [from_below, from_above], None)
    hidden_state = assembled(hidden_parts, columns)
    carried, hidden_state, below_b, above_b = lax.optimization_barrier(
        (carried, hidden_state, below_b, above_b)
    )
    far_a, far_b = along(below_a, 1), along(above_b, -1)
    middle = own_b + [from_below_other, from_above_other] + sum(ring.shared(below_b, above_b, 1), [])
    carried = expert(middle, carried)
    carried, far_a, far_b = lax.optimization_barrier((carried, far_a, far_b))
    hidden_rows = expert(ring.both(far_a, 2, 0) + ring.both(far_b, 2, 1), carried, model_width)
    hidden_rows = jnp.dot(turning, hidden_rows, preferred_element_type=F32).astype(BF16)
    return (hidden_state, hidden_rows[None])


def solution(mesh):
    placed = (
        P(("span", "expert"), None),
        P("span", "expert"),
        P("span", "expert"),
        P("span", "expert"),
        P("span", "expert"),
        P("span"),
        P("expert", "span"),
        P(),
        P(("span", "expert"), None),
        P("span", None, "expert"),
        P("span", None, "expert"),
    )
    return jax.shard_map(
        on_device,
        mesh=mesh,
        in_specs=placed,
        out_specs=(P(("span", "expert"), None), P("span", None, "expert")),
        check_vma=False,
    )
```

```python
import functools

import jax
import jax.numpy as jnp
from jax import lax
from jax.experimental import pallas as pl
from jax.experimental.pallas import tpu as pltpu
from jax.sharding import PartitionSpec as P

BLK = 512
EPSILON = 1e-05
HIGHEST = lax.Precision.HIGHEST
F32 = jnp.float32
BF16 = jnp.bfloat16
VMEM_LIMIT = 56 * 1024 * 1024
HEADS = 4
HD = 128
GRID_SIDE = 4


def whole(shape):
    return pl.BlockSpec(shape, lambda *_: (0,) * len(shape))


def smem():
    return pl.BlockSpec(memory_space=pltpu.SMEM)


def split_dot(a_f32, b_bf16):
    high = a_f32.astype(BF16)
    low = (a_f32 - high.astype(F32)).astype(BF16)
    return jnp.dot(high, b_bf16, preferred_element_type=F32) + jnp.dot(
        low, b_bf16, preferred_element_type=F32
    )


def state_kernel(start_ref, k_ref, v_ref, keep_ref, pay_ref, first_ref, thr_ref, cum_ref):
    start = start_ref[0]
    blocks = k_ref.shape[0] // BLK
    row = lax.broadcasted_iota(jnp.int32, (BLK, BLK), 0)
    col = lax.broadcasted_iota(jnp.int32, (BLK, BLK), 1)
    lower = (row >= col).astype(F32)
    place = lax.broadcasted_iota(jnp.int32, (BLK, HD), 0)
    through, tails = [], []
    for b in range(blocks):
        own = pl.ds(b * BLK, BLK)
        cum = jnp.dot(lower, keep_ref[own, :], precision=HIGHEST, preferred_element_type=F32)
        cum_ref[own, :] = cum
        end = cum[BLK - 1 :, :]
        here = start - b * BLK
        same = (place >= here) == (here <= BLK - 1)
        tails.append(jnp.where(same, jnp.exp(end - cum), 0.0))
        resets = (here >= 0) & (here < BLK)
        through.append(jnp.where(resets, 0.0, jnp.exp(end)))
    pay_ref[HEADS * HD :, :] = jnp.zeros_like(pay_ref[HEADS * HD :, :])
    thr_ref[...] = jnp.zeros_like(thr_ref)
    highs, lows = [], []
    for h in range(HEADS):
        lanes = slice(h * HD, (h + 1) * HD)
        state = None
        passed = jnp.ones((1, HD), F32)
        for b in range(blocks):
            own = pl.ds(b * BLK, BLK)
            key = k_ref[own, lanes].astype(F32) * tails[b][:, h : h + 1]
            added = split_dot(key.T, v_ref[own, lanes])
            thr = jnp.broadcast_to(through[b][:, h : h + 1], (1, HD))
            passed = passed * thr
            if b == 0:
                first_ref[lanes, :] = added
                thr_ref[h : h + 1, :] = thr
                state = added
            else:
                state = state * thr + added
        pay_ref[lanes, :] = state.astype(BF16)
        high = passed.astype(BF16)
        highs.append(high.astype(F32))
        lows.append(passed - high.astype(F32))
    none = jnp.zeros((8 - HEADS, HD), F32)
    pay_ref[HEADS * HD :, :] = jnp.concatenate(
        highs + [none] + lows + [none], axis=0
    ).astype(BF16)


def local_state(start, key_rows, values, keep_pad):
    tokens, width = key_rows.shape
    return pl.pallas_call(
        state_kernel,
        grid=(1,),
        in_specs=[smem(), whole((tokens, width)), whole((tokens, width)), whole((tokens, HD))],
        out_specs=[
            whole((width + 16, HD)),
            whole((width, HD)),
            whole((8, HD)),
            whole((tokens, HD)),
        ],
        out_shape=[
            jax.ShapeDtypeStruct((width + 16, HD), BF16),
            jax.ShapeDtypeStruct((width, HD), F32),
            jax.ShapeDtypeStruct((8, HD), F32),
            jax.ShapeDtypeStruct((tokens, HD), F32),
        ],
        compiler_params=pltpu.CompilerParams(vmem_limit_bytes=VMEM_LIMIT),
        cost_estimate=pl.CostEstimate(
            flops=2 * 10**9, bytes_accessed=4 * 10**6, transcendentals=10**5
        ),
        name="local_state",
    )(start, key_rows, values, keep_pad)


def intra_kernel(start_ref, q_ref, k_ref, v_ref, cum_ref, keep_t_ref, out_ref):
    start = start_ref[0]
    blocks = q_ref.shape[0] // BLK
    row = lax.broadcasted_iota(jnp.int32, (BLK, BLK), 0)
    col = lax.broadcasted_iota(jnp.int32, (BLK, BLK), 1)
    upper = (row <= col).astype(F32)
    part = BLK // 2
    for b in range(blocks):
        cum_t = jnp.dot(
            keep_t_ref[:, b * BLK : (b + 1) * BLK],
            upper,
            precision=HIGHEST,
            preferred_element_type=F32,
        )
        here = start - b * BLK
        for r in range(2):
            lo, n = r * part, (r + 1) * part
            t = lax.broadcasted_iota(jnp.int32, (part, n), 0) + lo
            s = lax.broadcasted_iota(jnp.int32, (part, n), 1)
            allowed = (t >= s) & ((s >= here) | (t < here))
            rows = pl.ds(b * BLK + lo, part)
            for h in range(HEADS):
                lanes = slice(h * HD, (h + 1) * HD)
                scores = lax.dot_general(
                    q_ref[rows, lanes],
                    k_ref[b * BLK : b * BLK + n, lanes],
                    (((1,), (1,)), ((), ())),
                    preferred_element_type=F32,
                )
                spread = cum_ref[rows, h : h + 1] - cum_t[h : h + 1, :n]
                decay = jnp.where(allowed, jnp.exp(jnp.where(allowed, spread, 0.0)), 0.0)
                weights = (scores * decay).astype(BF16)
                out_ref[rows, lanes] = jnp.dot(
                    weights, v_ref[b * BLK : b * BLK + n, lanes], preferred_element_type=F32
                )


def intra_part(start, queries, key_rows, values, cum, keep_t):
    tokens, width = queries.shape
    return pl.pallas_call(
        intra_kernel,
        grid=(1,),
        in_specs=[
            smem(),
            whole((tokens, width)),
            whole((tokens, width)),
            whole((tokens, width)),
            whole((tokens, HD)),
            whole((8, tokens)),
        ],
        out_specs=whole((tokens, width)),
        out_shape=jax.ShapeDtypeStruct((tokens, width), F32),
        compiler_params=pltpu.CompilerParams(vmem_limit_bytes=VMEM_LIMIT),
        cost_estimate=pl.CostEstimate(
            flops=8 * 10**9, bytes_accessed=6 * 10**6, transcendentals=2 * 10**6
        ),
        name="intra_part",
    )(start, queries, key_rows, values, cum, keep_t)


def passes_of(pay, h):
    base = HEADS * HD
    high = pay[base + h : base + h + 1, :].astype(F32)
    low = pay[base + 8 + h : base + 9 + h, :].astype(F32)
    return high + low


def row_kernel(place_ref, p0, p1, p2, p3, pay_ref, prefix_ref, through_ref):
    own = place_ref[0]
    parts = [p[...] for p in (p0, p1, p2, p3)]
    places = [lax.rem(own - d + GRID_SIDE, GRID_SIDE) for d in range(GRID_SIDE)]
    one = jnp.ones((1, HD), F32)
    through_ref[...] = jnp.zeros_like(through_ref)
    highs, lows = [], []
    for h in range(HEADS):
        lanes = slice(h * HD, (h + 1) * HD)
        thr = [passes_of(p, h) for p in parts]
        total = jnp.zeros((HD, HD), F32)
        prefix = jnp.zeros((HD, HD), F32)
        passed, before = one, one
        for d in range(GRID_SIDE):
            after, between = one, one
            for e in range(GRID_SIDE):
                if e == d:
                    continue
                later = places[e] > places[d]
                after = after * jnp.where(later, thr[e], one)
                between = between * jnp.where(later & (places[e] < own), thr[e], one)
            state = parts[d][lanes, :].astype(F32)
            total = total + state * after
            prefix = prefix + state * jnp.where(places[d] < own, between, 0.0 * one)
            passed = passed * thr[d]
            before = before * jnp.where(places[d] < own, thr[d], one)
        pay_ref[lanes, :] = total.astype(BF16)
        prefix_ref[lanes, :] = prefix
        through_ref[h : h + 1, :] = before
        high = passed.astype(BF16)
        highs.append(high.astype(F32))
        lows.append(passed - high.astype(F32))
    none = jnp.zeros((8 - HEADS, HD), F32)
    pay_ref[HEADS * HD :, :] = jnp.concatenate(
        highs + [none] + lows + [none], axis=0
    ).astype(BF16)


def row_states(place, parts):
    shape = parts[0].shape
    width = HEADS * HD
    return pl.pallas_call(
        row_kernel,
        grid=(1,),
        in_specs=[smem()] + [whole(shape)] * 4,
        out_specs=[whole(shape), whole((width, HD)), whole((8, HD))],
        out_shape=[
            jax.ShapeDtypeStruct(shape, BF16),
            jax.ShapeDtypeStruct((width, HD), F32),
            jax.ShapeDtypeStruct((8, HD), F32),
        ],
        cost_estimate=pl.CostEstimate(
            flops=10**6, bytes_accessed=10**6, transcendentals=0
        ),
        name="row_states",
    )(place, *parts)


def finish_kernel(
    start_ref, q_ref, intra_ref, cum_ref, e1, e2, e3, prefix_ref, before_ref, first_ref, thr_ref, *out_refs
):
    start = start_ref[0]
    blocks = q_ref.shape[0] // BLK
    rows1, rows2, rows3 = e1[...], e2[...], e3[...]
    place = lax.broadcasted_iota(jnp.int32, (BLK, HD), 0)
    factors = []
    for b in range(blocks):
        here = start - b * BLK
        opened = (place < here) | (here < 0)
        factors.append(jnp.where(opened, jnp.exp(cum_ref[pl.ds(b * BLK, BLK), :]), 0.0))
    for h in range(HEADS):
        lanes = slice(h * HD, (h + 1) * HD)
        far = rows2[lanes, :].astype(F32) + passes_of(rows2, h) * rows3[lanes, :].astype(F32)
        earlier = rows1[lanes, :].astype(F32) + passes_of(rows1, h) * far
        state = prefix_ref[lanes, :] + before_ref[h : h + 1, :] * earlier
        for b in range(blocks):
            own = pl.ds(b * BLK, BLK)
            if b > 0:
                state = state * thr_ref[h : h + 1, :] + first_ref[lanes, :]
            high = state.astype(BF16)
            low = (state - high.astype(F32)).astype(BF16)
            q = q_ref[own, lanes]
            carried = jnp.dot(q, high, preferred_element_type=F32) + jnp.dot(
                q, low, preferred_element_type=F32
            )
            heads = intra_ref[own, lanes] + carried * factors[b][:, h : h + 1]
            mean = jnp.mean(heads * heads, axis=1, keepdims=True)
            each = HEADS // 2
            half = slice(h % each * HD, (h % each + 1) * HD)
            out_refs[h // each][own, half] = (heads * lax.rsqrt(mean + EPSILON)).astype(BF16)


def finish(start, queries, intra, cum, rows, prefix, before, first, thr):
    tokens, width = queries.shape
    pay = rows[0].shape
    return pl.pallas_call(
        finish_kernel,
        grid=(1,),
        in_specs=[
            smem(),
            whole((tokens, width)),
            whole((tokens, width)),
            whole((tokens, HD)),
            whole(pay),
            whole(pay),
            whole(pay),
            whole((width, HD)),
            whole((8, HD)),
            whole((width, HD)),
            whole((8, HD)),
        ],
        out_specs=[whole((tokens, width // 2))] * 2,
        out_shape=[jax.ShapeDtypeStruct((tokens, width // 2), BF16)] * 2,
        compiler_params=pltpu.CompilerParams(vmem_limit_bytes=VMEM_LIMIT),
        cost_estimate=pl.CostEstimate(
            flops=10**9, bytes_accessed=5 * 10**6, transcendentals=10**6
        ),
        name="finish",
    )(start, queries, intra, cum, *rows, prefix, before, first, thr)


def proj_kernel(count, src_ref, *refs):
    xs = refs[:count]
    w_ref, res_ref, gain_ref, h_ref, x_ref = refs[count:]
    total = res_ref[...].astype(F32)
    for group in range(0, count, PROJ_GROUP):
        members = range(group, min(group + PROJ_GROUP, count))
        x = jnp.concatenate([xs[c][...] for c in members], axis=1)
        w = []
        for c in members:
            depth = xs[c].shape[1]
            at = pl.ds(pl.multiple_of(src_ref[c] * depth, depth), depth)
            w.append(w_ref[0, at, :])
        total = total + jnp.dot(x, jnp.concatenate(w, axis=0), preferred_element_type=F32)
    h_ref[...] = total.astype(BF16)
    x_ref[...] = (total * gain_ref[...]).astype(BF16)


PROJ_GROUP = 4


def project(src, xs, weights, res, gain, half):
    tokens = xs[0].shape[0]
    part = weights.shape[2]
    tile = tokens // 2
    rows = lambda width, at=0: pl.BlockSpec((tile, width), lambda n, s: (n, at))
    return pl.pallas_call(
        functools.partial(proj_kernel, len(xs)),
        grid_spec=pltpu.PrefetchScalarGridSpec(
            num_scalar_prefetch=1,
            grid=(tokens // tile,),
            in_specs=[rows(x.shape[1]) for x in xs]
            + [
                pl.BlockSpec((1,) + weights.shape[1:], lambda n, s: (half, 0, 0)),
                rows(part, half),
                pl.BlockSpec((1, part), lambda n, s: (0, half)),
            ],
            out_specs=[rows(part), rows(part)],
        ),
        out_shape=[jax.ShapeDtypeStruct((tokens, part), BF16)] * 2,
        compiler_params=pltpu.CompilerParams(vmem_limit_bytes=VMEM_LIMIT),
        cost_estimate=pl.CostEstimate(
            flops=2 * tokens * part * weights.shape[1],
            bytes_accessed=15 * 10**6,
            transcendentals=0,
        ),
        name="project",
    )(src, *xs, weights, res, gain)


NB = 128


def expert_kernel(count, begins, ends, steps, src_ref, *refs):
    xs = refs[:count]
    gates = refs[count : 2 * count]
    ups = refs[2 * count : 3 * count]
    inverses = refs[3 * count : 4 * count]
    rest = refs[4 * count :]
    if not begins:
        sum_in, squares_in = rest[:2]
        rest = rest[2:]
    if ends:
        out_ref, squares_ref = rest
    else:
        sum_out, squares_ref = rest

    def squared(rows):
        squares = None if begins else squares_in[rows, :]
        for c in range(count):
            plain = xs[c][rows, :].astype(F32) * inverses[c][...]
            plain = plain * plain
            for lane in range(plain.shape[1] // HD):
                part = plain[:, lane * HD : (lane + 1) * HD]
                squares = part if squares is None else squares + part
        return squares

    if ends:

        @pl.when(pl.program_id(0) == 0)
        def _():
            squares = squared(slice(None))
            mean = jnp.sum(squares, axis=1, keepdims=True) / ends
            squares_ref[...] = jnp.broadcast_to(lax.rsqrt(mean + EPSILON), squares.shape)

    else:
        share = xs[0].shape[0] // steps
        at = pl.ds(pl.multiple_of(pl.program_id(0) * share, share), share)
        squares_ref[at, :] = squared(at)

    x = jnp.concatenate([xs[c][...] for c in range(count)], axis=1)
    w = [jnp.concatenate([gates[c][...], ups[c][...]], axis=1) for c in range(count)]
    total = jnp.dot(x, jnp.concatenate(w, axis=0), preferred_element_type=F32)
    if not begins:
        total = total + sum_in[0]
    if ends:
        scale = squares_ref[...]
        gate, up = total[:, :NB] * scale, total[:, NB:] * scale
        out_ref[...] = (gate / (1.0 + jnp.exp(-gate)) * up).astype(BF16)
    else:
        sum_out[0] = total


def expert_part(src, xs, gate_w, up_w, inverse, carried, ends=0, place=0):
    tokens = min(x.shape[0] for x in xs)
    hidden = gate_w.shape[1]
    w_specs, i_specs = [], []
    for c, x in enumerate(xs):
        depth = x.shape[1]
        w_specs.append(pl.BlockSpec((depth, NB), lambda n, s, c=c: (s[c], n)))
        i_specs.append(pl.BlockSpec((1, depth), lambda n, s, c=c: (0, s[c])))
    x_specs = [
        pl.BlockSpec(
            (tokens, x.shape[1]), lambda n, s, at=place if x.shape[0] > tokens else 0: (at, 0)
        )
        for x in xs
    ]
    kept = [
        pl.BlockSpec((1, tokens, 2 * NB), lambda n, s: (n, place, 0)),
        pl.BlockSpec((tokens, HD), lambda n, s: (place, 0)),
    ]
    if ends:
        out_specs = pl.BlockSpec((tokens, NB), lambda n, s: (0, n))
        out_shape = jax.ShapeDtypeStruct((tokens, hidden), BF16)
        scratch = [pltpu.VMEM((tokens, HD), F32)]
    else:
        out_specs = kept
        out_shape = [
            jax.ShapeDtypeStruct((hidden // NB, tokens, 2 * NB), F32),
            jax.ShapeDtypeStruct((tokens, HD), F32),
        ]
        scratch = []
    count = len(xs)
    return pl.pallas_call(
        functools.partial(expert_kernel, count, carried is None, ends, hidden // NB),
        grid_spec=pltpu.PrefetchScalarGridSpec(
            num_scalar_prefetch=1,
            grid=(hidden // NB,),
            in_specs=x_specs
            + w_specs
            + w_specs
            + i_specs
            + ([] if carried is None else kept),
            out_specs=out_specs,
            scratch_shapes=scratch,
        ),
        out_shape=out_shape,
        compiler_params=pltpu.CompilerParams(vmem_limit_bytes=VMEM_LIMIT),
        cost_estimate=pl.CostEstimate(
            flops=4 * tokens * hidden * sum(x.shape[1] for x in xs),
            bytes_accessed=22 * 10**6,
            transcendentals=0,
        ),
        name="expert_part",
    )(
        src,
        *xs,
        *([gate_w] * count),
        *([up_w] * count),
        *([inverse] * count),
        *(() if carried is None else carried),
    )


def assemble_kernel(count, src_ref, *refs):
    out_ref = refs[count]
    for c in range(count):
        width = refs[c].shape[1]
        at = pl.ds(pl.multiple_of(src_ref[c] * width, width), width)
        out_ref[:, at] = refs[c][...]


def assembled(pairs, columns):
    parts, src = unzip(pairs)
    count = len(parts)
    rows = parts[0].shape[0]
    return pl.pallas_call(
        functools.partial(assemble_kernel, count),
        grid_spec=pltpu.PrefetchScalarGridSpec(
            num_scalar_prefetch=1,
            grid=(1,),
            in_specs=[whole(p.shape) for p in parts],
            out_specs=whole((rows, count * columns)),
        ),
        out_shape=jax.ShapeDtypeStruct((rows, count * columns), BF16),
        cost_estimate=pl.CostEstimate(
            flops=0, bytes_accessed=4 * rows * count * columns, transcendentals=0
        ),
        name="assembled",
    )(src, *parts)


def moved(block, axis, place_to):
    count = lax.axis_size(axis)
    return lax.ppermute(block, axis, [(i, place_to(i)) for i in range(count)])


def along(block, steps, cross=0):
    count = lax.axis_size("expert")
    return moved(block, "expert", lambda j: ((j // 2 + steps) * 2 + (j % 2 ^ cross)) % count)


class Ring:
    def __init__(self, me):
        self.count = lax.axis_size("expert")
        self.me, self.other = me, me + 1 - 2 * lax.rem(me, 2)

    def named(self, block, owner, steps, half):
        return block, 2 * lax.rem(owner + 2 * steps + self.count, self.count) + half

    def near(self, block, half):
        return (
            [self.named(block, self.me, 0, half), self.named(along(block, 0, 1), self.other, 0, half)],
            along(block, 1),
            along(block, -1),
        )

    def shared(self, below, above, half):
        return [
            self.both(below, -1, half),
            self.both(above, 1, half),
        ]

    def far(self, below, above, half):
        return self.both(along(above, -1) if half else along(below, 1), 2, half)

    def both(self, block, steps, half):
        return [
            self.named(block, self.me, steps, half),
            self.named(along(block, 0, 1), self.other, steps, half),
        ]


def returned(block, me):
    count = lax.axis_size("expert")
    rows = block.shape[0] // count
    parts = []
    for steps in range(count // 2):
        for cross in range(2):
            across = (1 - 2 * lax.rem(me, 2)) * cross
            to = lax.rem(me + across + 2 * steps, count)
            part = lax.dynamic_slice_in_dim(block, to * rows, rows, 0)
            if steps or cross:
                part = along(part, steps, cross)
            parts.append((part, lax.rem(me + across - 2 * steps + count, count)))
    return parts


def unzip(pairs):
    return [x for x, _ in pairs], jnp.stack([s for _, s in pairs]).astype(jnp.int32)


def on_device(
    residual_in,
    queries,
    key_rows,
    values,
    log_keep,
    prompt_start,
    out_proj,
    norm_gain,
    expert_ids,
    w_gate,
    w_up,
):
    tok_rows, model_width = residual_in.shape
    section_len = queries.shape[0]
    span_count = lax.axis_size("span")
    slice_count = lax.axis_size("expert")
    capacity = max(2, tok_rows * 5 // (4 * span_count))
    my_span = lax.axis_index("span")
    my_slice = lax.axis_index("expert")
    columns = model_width // slice_count

    pairs = []
    for i in range(span_count):
        for j in range(slice_count):
            pairs.append((i * slice_count + j, (i % 2 * slice_count + j) * slice_count + i // 2))
    piece = lax.ppermute(out_proj, ("span", "expert"), pairs)

    keep_pad = jnp.pad(log_keep, ((0, 0), (0, HD - log_keep.shape[1])))
    keep_t = jnp.pad(log_keep.T, ((0, 8 - log_keep.shape[1]), (0, 0)))
    pay, first, thr, cum = local_state(prompt_start, key_rows, values, keep_pad)
    side = GRID_SIDE
    in_row = [
        moved(pay, "span", lambda i, d=d: i // side * side + (i + d) % side)
        for d in range(1, side)
    ]
    piece, residual, *in_row = lax.optimization_barrier((piece, residual_in, *in_row))
    proj_w = lax.all_gather(piece, "span", axis=0)
    proj_w = proj_w.reshape(2, slice_count * out_proj.shape[0], out_proj.shape[1])
    named = jnp.broadcast_to(expert_ids.astype(BF16)[:, :, None], (tok_rows, slice_count, HD))
    res = jnp.concatenate([residual.reshape(tok_rows, slice_count, columns), named], axis=2)
    res = lax.all_to_all(res, "expert", split_axis=1, concat_axis=0, tiled=True)
    res = res.reshape(section_len, columns + HD)
    intra = intra_part(prompt_start, queries, key_rows, values, cum, keep_t)
    place = lax.rem(my_span, side)[None].astype(jnp.int32)
    row_pay, prefix, before = row_states(place, [pay] + in_row)
    rows = [
        lax.ppermute(
            row_pay,
            "span",
            [(i, i + d * side) for i in range(span_count) if i + d * side < span_count],
        )
        for d in range(1, side)
    ]
    normed = finish(prompt_start, queries, intra, cum, rows, prefix, before, first, thr)

    res, *normed = lax.optimization_barrier((res, *normed))
    ids = res[:, columns].astype(jnp.int32).reshape(slice_count, tok_rows)
    onehot = (ids[:, :, None] == jnp.arange(span_count)[None, None, :]).astype(BF16)
    earlier = jnp.tril(jnp.ones((tok_rows, tok_rows), BF16), -1)
    earlier_count = jnp.einsum("ts,bse->bte", earlier, onehot, preferred_element_type=F32)
    slot = jnp.sum(earlier_count * onehot.astype(F32), axis=2).astype(jnp.int32)
    block_of = jnp.arange(slice_count)[:, None]
    target = ((ids * slice_count + block_of) * capacity + slot).reshape(-1)
    slots = span_count * slice_count * capacity
    placing = (jnp.arange(slots)[:, None] == target[None, :]).astype(BF16)
    r = jnp.arange(slots)
    block, inner = r // (span_count * capacity), r % (span_count * capacity)
    wanted = (inner // capacity * slice_count + block) * capacity + inner % capacity
    turning = (wanted[:, None] == r[None, :]).astype(BF16)

    ring = Ring(my_slice)
    chunks, kept = [], []
    for half in range(2):
        own, below, above = ring.near(normed[half], half)
        chunks += own
        kept.append((below, above))
    for half in range(2):
        chunks += ring.far(*kept[half], half)
        chunks += sum(ring.shared(*kept[half], half), [])
    xs, src = unzip(chunks)
    gain_cols = lax.dynamic_slice_in_dim(norm_gain, my_slice * columns, columns)[None, :]
    placing, *xs = lax.optimization_barrier((placing, *xs))
    first_cols, first_rows = project(src, xs, proj_w, res, gain_cols, 0)
    second_cols, second_rows = project(src, xs, proj_w, res, gain_cols, 1)
    hidden_cols = jnp.concatenate([first_cols, second_cols], axis=1)

    def packed(rows):
        chosen = jnp.dot(placing, rows, preferred_element_type=F32).astype(BF16)
        return chosen.reshape(span_count, slice_count * capacity, columns // 2)

    def dispatched(rows):
        arrived = lax.all_to_all(rows, "span", split_axis=0, concat_axis=0, tiled=True)
        return arrived.reshape(slots, columns // 2)

    inverse = (1.0 / norm_gain)[None, :]
    gate_w, up_w = w_gate[0], w_up[0]

    def expert(group, carried, ends=0, place=0):
        xs, src = unzip(group)
        return expert_part(src, xs, gate_w, up_w, inverse, carried, ends, place)

    arrived_a, packed_b = lax.optimization_barrier(
        (dispatched(packed(first_rows)), packed(second_rows))
    )
    own_a, below_a, above_a = ring.near(arrived_a, 0)
    arrived_b = dispatched(packed_b)
    arrived_b, below_a, above_a = lax.optimization_barrier((arrived_b, below_a, above_a))
    own_b, below_b, above_b = ring.near(arrived_b, 1)
    (from_below, from_below_other), (from_above, from_above_other) = ring.shared(below_a, above_a, 0)
    carried = expert(own_a + [from_below, from_above], None)
    carried, turning, hidden_cols, below_b, above_b = lax.optimization_barrier(
        (carried, turning, hidden_cols, below_b, above_b)
    )
    far_a, far_b = along(below_a, 1), along(above_b, -1)
    middle = own_b + [from_below_other, from_above_other] + sum(ring.shared(below_b, above_b, 1), [])
    carried = expert(middle, carried)
    carried, hidden_cols, far_a, far_b = lax.optimization_barrier(
        (carried, hidden_cols, far_a, far_b)
    )
    hidden_parts = returned(hidden_cols, my_slice)
    hidden_rows = expert(ring.both(far_a, 2, 0) + ring.both(far_b, 2, 1), carried, model_width)
    hidden_rows, hidden_parts = lax.optimization_barrier((hidden_rows, hidden_parts))
    hidden_rows = jnp.dot(turning, hidden_rows, preferred_element_type=F32).astype(BF16)
    hidden_state = assembled(hidden_parts, columns)
    return (hidden_state, hidden_rows[None])


def solution(mesh):
    placed = (
        P(("span", "expert"), None),
        P("span", "expert"),
        P("span", "expert"),
        P("span", "expert"),
        P("span", "expert"),
        P("span"),
        P("expert", "span"),
        P(),
        P(("span", "expert"), None),
        P("span", None, "expert"),
        P("span", None, "expert"),
    )
    return jax.shard_map(
        on_device,
        mesh=mesh,
        in_specs=placed,
        out_specs=(P(("span", "expert"), None), P("span", None, "expert")),
        check_vma=False,
    )
```

```python
import functools

import jax
import jax.numpy as jnp
from jax import lax
from jax.experimental import pallas as pl
from jax.experimental.pallas import tpu as pltpu
from jax.sharding import PartitionSpec as P

BLK = 512
EPSILON = 1e-05
HIGHEST = lax.Precision.HIGHEST
F32 = jnp.float32
BF16 = jnp.bfloat16
VMEM_LIMIT = 56 * 1024 * 1024
HEADS = 4
HD = 128
GRID_SIDE = 4


def whole(shape):
    return pl.BlockSpec(shape, lambda *_: (0,) * len(shape))


def smem():
    return pl.BlockSpec(memory_space=pltpu.SMEM)


def split_dot(a_f32, b_bf16):
    high = a_f32.astype(BF16)
    low = (a_f32 - high.astype(F32)).astype(BF16)
    return jnp.dot(high, b_bf16, preferred_element_type=F32) + jnp.dot(
        low, b_bf16, preferred_element_type=F32
    )


def state_kernel(start_ref, k_ref, v_ref, keep_ref, pay_ref, first_ref, thr_ref, cum_ref):
    start = start_ref[0]
    blocks = k_ref.shape[0] // BLK
    row = lax.broadcasted_iota(jnp.int32, (BLK, BLK), 0)
    col = lax.broadcasted_iota(jnp.int32, (BLK, BLK), 1)
    lower = (row >= col).astype(F32)
    place = lax.broadcasted_iota(jnp.int32, (BLK, HD), 0)
    through, tails = [], []
    for b in range(blocks):
        own = pl.ds(b * BLK, BLK)
        cum = jnp.dot(lower, keep_ref[own, :], precision=HIGHEST, preferred_element_type=F32)
        cum_ref[own, :] = cum
        end = cum[BLK - 1 :, :]
        here = start - b * BLK
        same = (place >= here) == (here <= BLK - 1)
        tails.append(jnp.where(same, jnp.exp(end - cum), 0.0))
        resets = (here >= 0) & (here < BLK)
        through.append(jnp.where(resets, 0.0, jnp.exp(end)))
    pay_ref[HEADS * HD :, :] = jnp.zeros_like(pay_ref[HEADS * HD :, :])
    thr_ref[...] = jnp.zeros_like(thr_ref)
    highs, lows = [], []
    for h in range(HEADS):
        lanes = slice(h * HD, (h + 1) * HD)
        state = None
        passed = jnp.ones((1, HD), F32)
        for b in range(blocks):
            own = pl.ds(b * BLK, BLK)
            key = k_ref[own, lanes].astype(F32) * tails[b][:, h : h + 1]
            added = split_dot(key.T, v_ref[own, lanes])
            thr = jnp.broadcast_to(through[b][:, h : h + 1], (1, HD))
            passed = passed * thr
            if b == 0:
                first_ref[lanes, :] = added
                thr_ref[h : h + 1, :] = thr
                state = added
            else:
                state = state * thr + added
        pay_ref[lanes, :] = state.astype(BF16)
        high = passed.astype(BF16)
        highs.append(high.astype(F32))
        lows.append(passed - high.astype(F32))
    none = jnp.zeros((8 - HEADS, HD), F32)
    pay_ref[HEADS * HD :, :] = jnp.concatenate(
        highs + [none] + lows + [none], axis=0
    ).astype(BF16)


def local_state(start, key_rows, values, keep_pad):
    tokens, width = key_rows.shape
    return pl.pallas_call(
        state_kernel,
        grid=(1,),
        in_specs=[smem(), whole((tokens, width)), whole((tokens, width)), whole((tokens, HD))],
        out_specs=[
            whole((width + 16, HD)),
            whole((width, HD)),
            whole((8, HD)),
            whole((tokens, HD)),
        ],
        out_shape=[
            jax.ShapeDtypeStruct((width + 16, HD), BF16),
            jax.ShapeDtypeStruct((width, HD), F32),
            jax.ShapeDtypeStruct((8, HD), F32),
            jax.ShapeDtypeStruct((tokens, HD), F32),
        ],
        compiler_params=pltpu.CompilerParams(vmem_limit_bytes=VMEM_LIMIT),
        cost_estimate=pl.CostEstimate(
            flops=2 * 10**9, bytes_accessed=4 * 10**6, transcendentals=10**5
        ),
        name="local_state",
    )(start, key_rows, values, keep_pad)


def intra_kernel(start_ref, q_ref, k_ref, v_ref, cum_ref, keep_t_ref, out_ref):
    start = start_ref[0]
    blocks = q_ref.shape[0] // BLK
    row = lax.broadcasted_iota(jnp.int32, (BLK, BLK), 0)
    col = lax.broadcasted_iota(jnp.int32, (BLK, BLK), 1)
    upper = (row <= col).astype(F32)
    part = BLK // 2
    for b in range(blocks):
        cum_t = jnp.dot(
            keep_t_ref[:, b * BLK : (b + 1) * BLK],
            upper,
            precision=HIGHEST,
            preferred_element_type=F32,
        )
        here = start - b * BLK
        for r in range(2):
            lo, n = r * part, (r + 1) * part
            t = lax.broadcasted_iota(jnp.int32, (part, n), 0) + lo
            s = lax.broadcasted_iota(jnp.int32, (part, n), 1)
            allowed = (t >= s) & ((s >= here) | (t < here))
            rows = pl.ds(b * BLK + lo, part)
            for h in range(HEADS):
                lanes = slice(h * HD, (h + 1) * HD)
                scores = lax.dot_general(
                    q_ref[rows, lanes],
                    k_ref[b * BLK : b * BLK + n, lanes],
                    (((1,), (1,)), ((), ())),
                    preferred_element_type=F32,
                )
                spread = cum_ref[rows, h : h + 1] - cum_t[h : h + 1, :n]
                decay = jnp.where(allowed, jnp.exp(jnp.where(allowed, spread, 0.0)), 0.0)
                weights = (scores * decay).astype(BF16)
                out_ref[rows, lanes] = jnp.dot(
                    weights, v_ref[b * BLK : b * BLK + n, lanes], preferred_element_type=F32
                )


def intra_part(start, queries, key_rows, values, cum, keep_t):
    tokens, width = queries.shape
    return pl.pallas_call(
        intra_kernel,
        grid=(1,),
        in_specs=[
            smem(),
            whole((tokens, width)),
            whole((tokens, width)),
            whole((tokens, width)),
            whole((tokens, HD)),
            whole((8, tokens)),
        ],
        out_specs=whole((tokens, width)),
        out_shape=jax.ShapeDtypeStruct((tokens, width), F32),
        compiler_params=pltpu.CompilerParams(vmem_limit_bytes=VMEM_LIMIT),
        cost_estimate=pl.CostEstimate(
            flops=8 * 10**9, bytes_accessed=6 * 10**6, transcendentals=2 * 10**6
        ),
        name="intra_part",
    )(start, queries, key_rows, values, cum, keep_t)


def passes_of(pay, h):
    base = HEADS * HD
    high = pay[base + h : base + h + 1, :].astype(F32)
    low = pay[base + 8 + h : base + 9 + h, :].astype(F32)
    return high + low


def row_kernel(place_ref, p0, p1, p2, p3, pay_ref, prefix_ref, through_ref):
    own = place_ref[0]
    parts = [p[...] for p in (p0, p1, p2, p3)]
    places = [lax.rem(own - d + GRID_SIDE, GRID_SIDE) for d in range(GRID_SIDE)]
    one = jnp.ones((1, HD), F32)
    through_ref[...] = jnp.zeros_like(through_ref)
    highs, lows = [], []
    for h in range(HEADS):
        lanes = slice(h * HD, (h + 1) * HD)
        thr = [passes_of(p, h) for p in parts]
        total = jnp.zeros((HD, HD), F32)
        prefix = jnp.zeros((HD, HD), F32)
        passed, before = one, one
        for d in range(GRID_SIDE):
            after, between = one, one
            for e in range(GRID_SIDE):
                if e == d:
                    continue
                later = places[e] > places[d]
                after = after * jnp.where(later, thr[e], one)
                between = between * jnp.where(later & (places[e] < own), thr[e], one)
            state = parts[d][lanes, :].astype(F32)
            total = total + state * after
            prefix = prefix + state * jnp.where(places[d] < own, between, 0.0 * one)
            passed = passed * thr[d]
            before = before * jnp.where(places[d] < own, thr[d], one)
        pay_ref[lanes, :] = total.astype(BF16)
        prefix_ref[lanes, :] = prefix
        through_ref[h : h + 1, :] = before
        high = passed.astype(BF16)
        highs.append(high.astype(F32))
        lows.append(passed - high.astype(F32))
    none = jnp.zeros((8 - HEADS, HD), F32)
    pay_ref[HEADS * HD :, :] = jnp.concatenate(
        highs + [none] + lows + [none], axis=0
    ).astype(BF16)


def row_states(place, parts):
    shape = parts[0].shape
    width = HEADS * HD
    return pl.pallas_call(
        row_kernel,
        grid=(1,),
        in_specs=[smem()] + [whole(shape)] * 4,
        out_specs=[whole(shape), whole((width, HD)), whole((8, HD))],
        out_shape=[
            jax.ShapeDtypeStruct(shape, BF16),
            jax.ShapeDtypeStruct((width, HD), F32),
            jax.ShapeDtypeStruct((8, HD), F32),
        ],
        cost_estimate=pl.CostEstimate(
            flops=10**6, bytes_accessed=10**6, transcendentals=0
        ),
        name="row_states",
    )(place, *parts)


def finish_kernel(
    start_ref, q_ref, intra_ref, cum_ref, e1, e2, e3, prefix_ref, before_ref, first_ref, thr_ref, *out_refs
):
    start = start_ref[0]
    blocks = q_ref.shape[0] // BLK
    rows1, rows2, rows3 = e1[...], e2[...], e3[...]
    place = lax.broadcasted_iota(jnp.int32, (BLK, HD), 0)
    factors = []
    for b in range(blocks):
        here = start - b * BLK
        opened = (place < here) | (here < 0)
        factors.append(jnp.where(opened, jnp.exp(cum_ref[pl.ds(b * BLK, BLK), :]), 0.0))
    for h in range(HEADS):
        lanes = slice(h * HD, (h + 1) * HD)
        far = rows2[lanes, :].astype(F32) + passes_of(rows2, h) * rows3[lanes, :].astype(F32)
        earlier = rows1[lanes, :].astype(F32) + passes_of(rows1, h) * far
        state = prefix_ref[lanes, :] + before_ref[h : h + 1, :] * earlier
        for b in range(blocks):
            own = pl.ds(b * BLK, BLK)
            if b > 0:
                state = state * thr_ref[h : h + 1, :] + first_ref[lanes, :]
            high = state.astype(BF16)
            low = (state - high.astype(F32)).astype(BF16)
            q = q_ref[own, lanes]
            carried = jnp.dot(q, high, preferred_element_type=F32) + jnp.dot(
                q, low, preferred_element_type=F32
            )
            heads = intra_ref[own, lanes] + carried * factors[b][:, h : h + 1]
            mean = jnp.mean(heads * heads, axis=1, keepdims=True)
            each = HEADS // 2
            half = slice(h % each * HD, (h % each + 1) * HD)
            out_refs[h // each][own, half] = (heads * lax.rsqrt(mean + EPSILON)).astype(BF16)


def finish(start, queries, intra, cum, rows, prefix, before, first, thr):
    tokens, width = queries.shape
    pay = rows[0].shape
    return pl.pallas_call(
        finish_kernel,
        grid=(1,),
        in_specs=[
            smem(),
            whole((tokens, width)),
            whole((tokens, width)),
            whole((tokens, HD)),
            whole(pay),
            whole(pay),
            whole(pay),
            whole((width, HD)),
            whole((8, HD)),
            whole((width, HD)),
            whole((8, HD)),
        ],
        out_specs=[whole((tokens, width // 2))] * 2,
        out_shape=[jax.ShapeDtypeStruct((tokens, width // 2), BF16)] * 2,
        compiler_params=pltpu.CompilerParams(vmem_limit_bytes=VMEM_LIMIT),
        cost_estimate=pl.CostEstimate(
            flops=10**9, bytes_accessed=5 * 10**6, transcendentals=10**6
        ),
        name="finish",
    )(start, queries, intra, cum, *rows, prefix, before, first, thr)


def proj_kernel(count, src_ref, *refs):
    xs = refs[:count]
    w_ref, res_ref, gain_ref, h_ref, x_ref = refs[count:]
    total = res_ref[...].astype(F32)
    for group in range(0, count, PROJ_GROUP):
        members = range(group, min(group + PROJ_GROUP, count))
        x = jnp.concatenate([xs[c][...] for c in members], axis=1)
        w = []
        for c in members:
            depth = xs[c].shape[1]
            at = pl.ds(pl.multiple_of(src_ref[c] * depth, depth), depth)
            w.append(w_ref[0, at, :])
        total = total + jnp.dot(x, jnp.concatenate(w, axis=0), preferred_element_type=F32)
    h_ref[...] = total.astype(BF16)
    x_ref[...] = (total * gain_ref[...]).astype(BF16)


PROJ_GROUP = 4


def project(src, xs, weights, res, gain, half):
    tokens = xs[0].shape[0]
    part = weights.shape[2]
    tile = tokens // 2
    rows = lambda width, at=0: pl.BlockSpec((tile, width), lambda n, s: (n, at))
    return pl.pallas_call(
        functools.partial(proj_kernel, len(xs)),
        grid_spec=pltpu.PrefetchScalarGridSpec(
            num_scalar_prefetch=1,
            grid=(tokens // tile,),
            in_specs=[rows(x.shape[1]) for x in xs]
            + [
                pl.BlockSpec((1,) + weights.shape[1:], lambda n, s: (half, 0, 0)),
                rows(part, half),
                pl.BlockSpec((1, part), lambda n, s: (0, half)),
            ],
            out_specs=[rows(part), rows(part)],
        ),
        out_shape=[jax.ShapeDtypeStruct((tokens, part), BF16)] * 2,
        compiler_params=pltpu.CompilerParams(vmem_limit_bytes=VMEM_LIMIT),
        cost_estimate=pl.CostEstimate(
            flops=2 * tokens * part * weights.shape[1],
            bytes_accessed=15 * 10**6,
            transcendentals=0,
        ),
        name="project",
    )(src, *xs, weights, res, gain)


NB = 128


def expert_kernel(count, begins, ends, steps, src_ref, *refs):
    xs = refs[:count]
    gates = refs[count : 2 * count]
    ups = refs[2 * count : 3 * count]
    inverses = refs[3 * count : 4 * count]
    rest = refs[4 * count :]
    if not begins:
        sum_in, squares_in = rest[:2]
        rest = rest[2:]
    if ends:
        out_ref, squares_ref = rest
    else:
        sum_out, squares_ref = rest

    def squared(rows):
        squares = None if begins else squares_in[rows, :]
        for c in range(count):
            plain = xs[c][rows, :].astype(F32) * inverses[c][...]
            plain = plain * plain
            for lane in range(plain.shape[1] // HD):
                part = plain[:, lane * HD : (lane + 1) * HD]
                squares = part if squares is None else squares + part
        return squares

    if ends:

        @pl.when(pl.program_id(0) == 0)
        def _():
            squares = squared(slice(None))
            mean = jnp.sum(squares, axis=1, keepdims=True) / ends
            squares_ref[...] = jnp.broadcast_to(lax.rsqrt(mean + EPSILON), squares.shape)

    else:
        share = xs[0].shape[0] // steps
        at = pl.ds(pl.multiple_of(pl.program_id(0) * share, share), share)
        squares_ref[at, :] = squared(at)

    x = jnp.concatenate([xs[c][...] for c in range(count)], axis=1)
    w = [jnp.concatenate([gates[c][...], ups[c][...]], axis=1) for c in range(count)]
    total = jnp.dot(x, jnp.concatenate(w, axis=0), preferred_element_type=F32)
    if not begins:
        total = total + sum_in[0]
    if ends:
        scale = squares_ref[...]
        gate, up = total[:, :NB] * scale, total[:, NB:] * scale
        out_ref[...] = (gate / (1.0 + jnp.exp(-gate)) * up).astype(BF16)
    else:
        sum_out[0] = total


def expert_part(src, xs, gate_w, up_w, inverse, carried, ends=0, place=0):
    tokens = min(x.shape[0] for x in xs)
    hidden = gate_w.shape[1]
    w_specs, i_specs = [], []
    for c, x in enumerate(xs):
        depth = x.shape[1]
        w_specs.append(pl.BlockSpec((depth, NB), lambda n, s, c=c: (s[c], n)))
        i_specs.append(pl.BlockSpec((1, depth), lambda n, s, c=c: (0, s[c])))
    x_specs = [
        pl.BlockSpec(
            (tokens, x.shape[1]), lambda n, s, at=place if x.shape[0] > tokens else 0: (at, 0)
        )
        for x in xs
    ]
    kept = [
        pl.BlockSpec((1, tokens, 2 * NB), lambda n, s: (n, place, 0)),
        pl.BlockSpec((tokens, HD), lambda n, s: (place, 0)),
    ]
    if ends:
        out_specs = pl.BlockSpec((tokens, NB), lambda n, s: (0, n))
        out_shape = jax.ShapeDtypeStruct((tokens, hidden), BF16)
        scratch = [pltpu.VMEM((tokens, HD), F32)]
    else:
        out_specs = kept
        out_shape = [
            jax.ShapeDtypeStruct((hidden // NB, tokens, 2 * NB), F32),
            jax.ShapeDtypeStruct((tokens, HD), F32),
        ]
        scratch = []
    count = len(xs)
    return pl.pallas_call(
        functools.partial(expert_kernel, count, carried is None, ends, hidden // NB),
        grid_spec=pltpu.PrefetchScalarGridSpec(
            num_scalar_prefetch=1,
            grid=(hidden // NB,),
            in_specs=x_specs
            + w_specs
            + w_specs
            + i_specs
            + ([] if carried is None else kept),
            out_specs=out_specs,
            scratch_shapes=scratch,
        ),
        out_shape=out_shape,
        compiler_params=pltpu.CompilerParams(vmem_limit_bytes=VMEM_LIMIT),
        cost_estimate=pl.CostEstimate(
            flops=4 * tokens * hidden * sum(x.shape[1] for x in xs),
            bytes_accessed=22 * 10**6,
            transcendentals=0,
        ),
        name="expert_part",
    )(
        src,
        *xs,
        *([gate_w] * count),
        *([up_w] * count),
        *([inverse] * count),
        *(() if carried is None else carried),
    )


def assemble_kernel(count, src_ref, *refs):
    out_ref = refs[count]
    for c in range(count):
        width = refs[c].shape[1]
        at = pl.ds(pl.multiple_of(src_ref[c] * width, width), width)
        out_ref[:, at] = refs[c][...]


def assembled(pairs, columns):
    parts, src = unzip(pairs)
    count = len(parts)
    rows = parts[0].shape[0]
    return pl.pallas_call(
        functools.partial(assemble_kernel, count),
        grid_spec=pltpu.PrefetchScalarGridSpec(
            num_scalar_prefetch=1,
            grid=(1,),
            in_specs=[whole(p.shape) for p in parts],
            out_specs=whole((rows, count * columns)),
        ),
        out_shape=jax.ShapeDtypeStruct((rows, count * columns), BF16),
        cost_estimate=pl.CostEstimate(
            flops=0, bytes_accessed=4 * rows * count * columns, transcendentals=0
        ),
        name="assembled",
    )(src, *parts)


def moved(block, axis, place_to):
    count = lax.axis_size(axis)
    return lax.ppermute(block, axis, [(i, place_to(i)) for i in range(count)])


def along(block, steps, cross=0):
    count = lax.axis_size("expert")
    return moved(block, "expert", lambda j: ((j // 2 + steps) * 2 + (j % 2 ^ cross)) % count)


class Ring:
    def __init__(self, me):
        self.count = lax.axis_size("expert")
        self.me, self.other = me, me + 1 - 2 * lax.rem(me, 2)

    def named(self, block, owner, steps, half):
        return block, 2 * lax.rem(owner + 2 * steps + self.count, self.count) + half

    def near(self, block, half):
        return (
            [self.named(block, self.me, 0, half), self.named(along(block, 0, 1), self.other, 0, half)],
            along(block, 1),
            along(block, -1),
        )

    def shared(self, below, above, half):
        return [
            self.both(below, -1, half),
            self.both(above, 1, half),
        ]

    def far(self, below, above, half):
        return self.both(along(above, -1) if half else along(below, 1), 2, half)

    def both(self, block, steps, half):
        return [
            self.named(block, self.me, steps, half),
            self.named(along(block, 0, 1), self.other, steps, half),
        ]


def returned(block, me):
    count = lax.axis_size("expert")
    rows = block.shape[0] // count
    parts = []
    for steps in range(count // 2):
        for cross in range(2):
            across = (1 - 2 * lax.rem(me, 2)) * cross
            to = lax.rem(me + across + 2 * steps, count)
            part = lax.dynamic_slice_in_dim(block, to * rows, rows, 0)
            if steps or cross:
                part = along(part, steps, cross)
            parts.append((part, lax.rem(me + across - 2 * steps + count, count)))
    return parts


def unzip(pairs):
    return [x for x, _ in pairs], jnp.stack([s for _, s in pairs]).astype(jnp.int32)


def on_device(
    residual_in,
    queries,
    key_rows,
    values,
    log_keep,
    prompt_start,
    out_proj,
    norm_gain,
    expert_ids,
    w_gate,
    w_up,
):
    tok_rows, model_width = residual_in.shape
    section_len = queries.shape[0]
    span_count = lax.axis_size("span")
    slice_count = lax.axis_size("expert")
    capacity = max(2, tok_rows * 5 // (4 * span_count))
    my_span = lax.axis_index("span")
    my_slice = lax.axis_index("expert")
    columns = model_width // slice_count

    pairs = []
    for i in range(span_count):
        for j in range(slice_count):
            pairs.append((i * slice_count + j, (i % 2 * slice_count + j) * slice_count + i // 2))
    piece = lax.ppermute(out_proj, ("span", "expert"), pairs)

    keep_pad = jnp.pad(log_keep, ((0, 0), (0, HD - log_keep.shape[1])))
    keep_t = jnp.pad(log_keep.T, ((0, 8 - log_keep.shape[1]), (0, 0)))
    pay, first, thr, cum = local_state(prompt_start, key_rows, values, keep_pad)
    side = GRID_SIDE
    in_row = [
        moved(pay, "span", lambda i, d=d: i // side * side + (i + d) % side)
        for d in range(1, side)
    ]
    piece, residual, *in_row = lax.optimization_barrier((piece, residual_in, *in_row))
    proj_w = lax.all_gather(piece, "span", axis=0)
    proj_w = proj_w.reshape(2, slice_count * out_proj.shape[0], out_proj.shape[1])
    named = jnp.broadcast_to(expert_ids.astype(BF16)[:, :, None], (tok_rows, slice_count, HD))
    res = jnp.concatenate([residual.reshape(tok_rows, slice_count, columns), named], axis=2)
    res = lax.all_to_all(res, "expert", split_axis=1, concat_axis=0, tiled=True)
    res = res.reshape(section_len, columns + HD)
    intra = intra_part(prompt_start, queries, key_rows, values, cum, keep_t)
    place = lax.rem(my_span, side)[None].astype(jnp.int32)
    row_pay, prefix, before = row_states(place, [pay] + in_row)
    rows = [
        lax.ppermute(
            row_pay,
            "span",
            [(i, i + d * side) for i in range(span_count) if i + d * side < span_count],
        )
        for d in range(1, side)
    ]
    normed = finish(prompt_start, queries, intra, cum, rows, prefix, before, first, thr)

    res, *normed = lax.optimization_barrier((res, *normed))
    ids = res[:, columns].astype(jnp.int32).reshape(slice_count, tok_rows)
    onehot = (ids[:, :, None] == jnp.arange(span_count)[None, None, :]).astype(BF16)
    earlier = jnp.tril(jnp.ones((tok_rows, tok_rows), BF16), -1)
    earlier_count = jnp.einsum("ts,bse->bte", earlier, onehot, preferred_element_type=F32)
    slot = jnp.sum(earlier_count * onehot.astype(F32), axis=2).astype(jnp.int32)
    block_of = jnp.arange(slice_count)[:, None]
    target = ((ids * slice_count + block_of) * capacity + slot).reshape(-1)
    slots = span_count * slice_count * capacity
    placing = (jnp.arange(slots)[:, None] == target[None, :]).astype(BF16)
    r = jnp.arange(slots)
    block, inner = r // (span_count * capacity), r % (span_count * capacity)
    wanted = (inner // capacity * slice_count + block) * capacity + inner % capacity
    turning = (wanted[:, None] == r[None, :]).astype(BF16)

    ring = Ring(my_slice)
    chunks, kept = [], []
    for half in range(2):
        own, below, above = ring.near(normed[half], half)
        chunks += own
        kept.append((below, above))
    for half in range(2):
        chunks += ring.far(*kept[half], half)
        chunks += sum(ring.shared(*kept[half], half), [])
    xs, src = unzip(chunks)
    gain_cols = lax.dynamic_slice_in_dim(norm_gain, my_slice * columns, columns)[None, :]
    placing, *xs = lax.optimization_barrier((placing, *xs))
    first_cols, first_rows = project(src, xs, proj_w, res, gain_cols, 0)
    second_cols, second_rows = project(src, xs, proj_w, res, gain_cols, 1)
    hidden_cols = jnp.concatenate([first_cols, second_cols], axis=1)

    def packed(rows):
        chosen = jnp.dot(placing, rows, preferred_element_type=F32).astype(BF16)
        return chosen.reshape(span_count, slice_count * capacity, columns // 2)

    def dispatched(rows):
        arrived = lax.all_to_all(rows, "span", split_axis=0, concat_axis=0, tiled=True)
        return arrived.reshape(slots, columns // 2)

    inverse = (1.0 / norm_gain)[None, :]
    gate_w, up_w = w_gate[0], w_up[0]

    def expert(group, carried, ends=0, place=0):
        xs, src = unzip(group)
        return expert_part(src, xs, gate_w, up_w, inverse, carried, ends, place)

    arrived_a, packed_b = lax.optimization_barrier(
        (dispatched(packed(first_rows)), packed(second_rows))
    )
    own_a, below_a, above_a = ring.near(arrived_a, 0)
    arrived_b = dispatched(packed_b)
    arrived_b, below_a, above_a = lax.optimization_barrier((arrived_b, below_a, above_a))
    own_b, below_b, above_b = ring.near(arrived_b, 1)
    (from_below, from_below_other), (from_above, from_above_other) = ring.shared(below_a, above_a, 0)
    carried = expert(own_a + [from_below, from_above], None)
    carried, hidden_cols, below_b, above_b = lax.optimization_barrier(
        (carried, hidden_cols, below_b, above_b)
    )
    far_a, far_b = along(below_a, 1), along(above_b, -1)
    middle = own_b + [from_below_other, from_above_other] + sum(ring.shared(below_b, above_b, 1), [])
    carried = expert(middle, carried)
    carried, hidden_cols, far_a, far_b = lax.optimization_barrier(
        (carried, hidden_cols, far_a, far_b)
    )
    hidden_parts = returned(hidden_cols, my_slice)
    hidden_rows = expert(ring.both(far_a, 2, 0) + ring.both(far_b, 2, 1), carried, model_width)
    hidden_rows = jnp.dot(turning, hidden_rows, preferred_element_type=F32).astype(BF16)
    hidden_rows, hidden_parts = lax.optimization_barrier((hidden_rows, hidden_parts))
    hidden_state = assembled(hidden_parts, columns)
    return (hidden_state, hidden_rows[None])


def solution(mesh):
    placed = (
        P(("span", "expert"), None),
        P("span", "expert"),
        P("span", "expert"),
        P("span", "expert"),
        P("span", "expert"),
        P("span"),
        P("expert", "span"),
        P(),
        P(("span", "expert"), None),
        P("span", None, "expert"),
        P("span", None, "expert"),
    )
    return jax.shard_map(
        on_device,
        mesh=mesh,
        in_specs=placed,
        out_specs=(P(("span", "expert"), None), P("span", None, "expert")),
        check_vma=False,
    )
```
